128 devices in a mesh: dp: 8 (over z_lo, y), mp: 16 (over z_hi, x, core).
Axes of the slice: x: 4, y: 4, z: 4 (z_hi: 2, z_lo: 2; z = z_hi * 2 + z_lo), core: 2. Of those that a mesh axis runs over, the one named last changes fastest.
Arguments:
- tokens: bfloat16 [5120, 4096], P(('dp', 'mp')), may hold values from -24 to 24
- w_gate: bfloat16 [4096, 8192], P(None, 'mp'), may hold values from -0.09375 to 0.09375
- w_up: bfloat16 [4096, 8192], P(None, 'mp'), may hold values from -0.09375 to 0.09375
- w_down: bfloat16 [8192, 4096], P('mp'), may hold values from -0.0625 to 0.0625
- cotangent: bfloat16 [5120, 4096], P(('dp', 'mp')), may hold values from -6 to 6
Outputs:
- mixed: bfloat16 [5120, 4096], P(('dp', 'mp'))
- input_grad: bfloat16 [5120, 4096], P(('dp', 'mp'))
- grad_gate: bfloat16 [4096, 8192], P('dp', 'mp')
- grad_up: bfloat16 [4096, 8192], P('dp', 'mp')
- grad_down: bfloat16 [8192, 4096], P('mp', 'dp')
The draws below stay inside these ranges and needn't reach their ends.
All inputs are finite; a program needn't handle non-finite values.
Results may differ from the reference program's by a relative error of at most 0.019.
Values may be sent and summed in bfloat16 or wider, within the bound.
A program may use at most 192 MiB of HBM per device.

```python
import jax
import jax.numpy as jnp
from jax import lax

D = 4096
FF = 8192
TOKENS = 5120
N_DP = 8


def strengthened(drawn, stream_key, source, target, parts, factor):
    owner, partner = [(jnp.arange(drawn.shape[dim]) // (drawn.shape[dim] // parts)).reshape([-1 if axis == dim else 1 for axis in range(drawn.ndim)]) for dim in (source, target)]
    chosen = jax.random.permutation(stream_key, parts)[partner]
    strong = (owner == chosen) | (owner == (partner + parts // 2) % parts)
    return jnp.where(strong, factor * drawn, drawn)


def steps_of(rng, dims, pieces, smallest, largest):
    level, own = 1.0, jax.random.fold_in(rng, 6)
    for axis_at, shards_of in pieces:
        heights = jnp.exp(jax.random.uniform(jax.random.fold_in(own, axis_at), (shards_of,), jnp.float32, smallest / len(pieces), largest / len(pieces)))
        level = level * jnp.repeat(heights, dims[axis_at] // shards_of).reshape([-1 if axis == axis_at else 1 for axis in range(len(dims))])
    return level


def centred(own_key, extent, width, most, cuts=(), held_as=jnp.bfloat16):
    drawn = width * jax.random.normal(own_key, extent, jnp.float32)
    if cuts:
        drawn = drawn * steps_of(own_key, extent, cuts, -0.22, 0.18)
    return jnp.clip(drawn, -most, most).astype(held_as)


def gaussian_with(stream_key, shape, spread, most, split, heavy, dtype=jnp.bfloat16):
    entries = spread * jax.random.normal(stream_key, shape, jnp.float32)
    if split:
        entries = entries * steps_of(stream_key, shape, split, -0.22, 0.18)
    return jnp.clip(strengthened(entries, jax.random.fold_in(stream_key, 3), *heavy), -most, most).astype(dtype)


def setup_inputs(seed: int = 0) -> dict:
    seeds = jax.random.split(jax.random.key(seed), 6)
    tokens = gaussian_with(seeds[0], (TOKENS, D), 1.0, 24.0, ((0, 128),), (0, 1, 128, 5.5))
    w_gate = centred(seeds[1], (D, FF), D ** -0.5, 0.09375, ((1, 16),))
    w_up = centred(seeds[2], (D, FF), D ** -0.5, 0.09375, ((1, 16),))
    w_down = centred(seeds[3], (FF, D), FF ** -0.5, 0.0625, ((0, 16),))
    cotangent = centred(seeds[4], (TOKENS, D), 1.0, 6.0, ((0, 128),))
    return {"tokens": tokens, "w_gate": w_gate, "w_up": w_up, "w_down": w_down, "cotangent": cotangent}


def group_sum(left, right):
    width_left = left.shape[1]
    width_right = right.shape[1]
    left_groups = left.reshape(N_DP, -1, width_left)
    right_groups = right.reshape(N_DP, -1, width_right)

    def step(total, pair):
        term = jnp.dot(pair[0].T, pair[1], preferred_element_type=jnp.float32)
        term = lax.optimization_barrier(term.astype(jnp.bfloat16)).astype(jnp.float32)
        return total + term, None

    total, unused = lax.scan(step, jnp.zeros((width_left, width_right), jnp.float32), (left_groups, right_groups))
    return total.astype(jnp.bfloat16)


def reference(tokens, w_gate, w_up, w_down, cotangent):
    gate = jnp.dot(tokens, w_gate, preferred_element_type=jnp.float32)
    up = jnp.dot(tokens, w_up, preferred_element_type=jnp.float32)
    swish = jax.nn.silu(gate)
    hidden = (swish * up).astype(jnp.bfloat16)
    mixed = jnp.dot(hidden, w_down, preferred_element_type=jnp.float32).astype(jnp.bfloat16)
    dhidden = jnp.dot(cotangent, w_down.T, preferred_element_type=jnp.float32)
    sigma = jax.nn.sigmoid(gate)
    dgate = (dhidden * up * sigma * (1.0 + gate * (1.0 - sigma))).astype(jnp.bfloat16)
    dup = (dhidden * swish).astype(jnp.bfloat16)
    input_grad = (jnp.dot(dgate, w_gate.T, preferred_element_type=jnp.float32)
                  + jnp.dot(dup, w_up.T, preferred_element_type=jnp.float32)).astype(jnp.bfloat16)
    grad_gate = group_sum(tokens, dgate)
    grad_up = group_sum(tokens, dup)
    grad_down = group_sum(hidden, cotangent)
    return mixed, input_grad, grad_gate, grad_up, grad_down
```

```python
import jax
import jax.numpy as jnp
from jax import lax
from jax.experimental import pallas as pl
from jax.experimental.pallas import tpu as pltpu
from jax.sharding import PartitionSpec as P

MESH = pl.DeviceIdType.MESH
BF16 = jnp.bfloat16
F32 = jnp.float32
D = 4096
HALF = D // 2
LANE = HALF // 2
PANEL = 512
ROWS = 640
BLOCK = 80
PART = 320
MESSAGES = 110

OWN, LEFT, RIGHT, ACROSS, FAR, ACROSS_LEFT, ACROSS_RIGHT, ACROSS_FAR = range(8)


def mm(a, b):
    return jnp.dot(a, b, preferred_element_type=F32)


def mm_nt(a, b):
    return lax.dot_general(a, b, (((1,), (1,)), ((), ())), preferred_element_type=F32)


def add_into(dst, src, rows, step):
    @pl.loop(0, rows // step)
    def _(i):
        r = pl.ds(pl.multiple_of(i * step, step), step)
        dst[r, :] = (dst[r, :].astype(F32) + src[r, :].astype(F32)).astype(BF16)


def sum_to(dst, terms, rows, step):
    @pl.loop(0, rows // step)
    def _(i):
        r = pl.ds(pl.multiple_of(i * step, step), step)
        total = terms[0][r, :].astype(F32)
        for term in terms[1:]:
            total += term[r, :].astype(F32)
        dst[r, :] = total.astype(BF16)


def kernel(
    tok_hbm, wg_hbm, wu_hbm, wd_hbm, cot_hbm,
    mixed_out, ig_out, gate_out, up_out, down_out,
    wg, wu, wd, xc, hid, dg, du, lt, gf, uf, df, am, sm, pgu, pdo,
    mring, mz, gring, gz, dz, dring, t_in, fo,
    send_sem, recv_sem, local_sem, credit,
):
    dp, mp = lax.axis_index("dp"), lax.axis_index("mp")
    zl, y = dp // 4, dp % 4
    zh, x, c = mp // 8, (mp // 2) % 4, mp % 2
    x_right = (dp, zh * 8 + ((x + 1) % 4) * 2 + c)
    x_left = (dp, zh * 8 + ((x + 3) % 4) * 2 + c)
    z_across = (dp, (1 - zh) * 8 + x * 2 + c)
    sibling = (dp, zh * 8 + x * 2 + (1 - c))
    y_right = (zl * 4 + (y + 1) % 4, mp)
    y_left = (zl * 4 + (y + 3) % 4, mp)
    z_next = ((1 - zl) * 4 + y, mp)
    mine = pl.ds(pl.multiple_of(c * HALF, HALF), HALF)
    other = pl.ds(pl.multiple_of((1 - c) * HALF, HALF), HALF)

    pending = []

    def message(src, dst, device):
        n = len(pending)
        copy = pltpu.make_async_remote_copy(
            src_ref=src, dst_ref=dst, send_sem=send_sem.at[n], recv_sem=recv_sem.at[n],
            device_id=device, device_id_type=MESH,
        )
        pending.append(copy)
        return copy

    sent = set()

    def wait_send(copy):
        if id(copy) not in sent:
            sent.add(id(copy))
            copy.wait_send()

    weights = [
        pltpu.make_async_copy(src, dst, local_sem.at[n])
        for n, (src, dst) in enumerate(((wg_hbm, wg), (wu_hbm, wu), (wd_hbm, wd)))
    ]
    inputs = (tok_hbm, cot_hbm)
    own_rows = [pltpu.make_async_copy(inputs[a].at[:, mine], t_in.at[c, a], local_sem.at[3 + a]) for a in (0, 1)]
    for copy in own_rows:
        copy.start()
    for copy in weights:
        copy.start()

    barrier = pltpu.get_barrier_semaphore()
    partners = (x_right, x_left, z_across, sibling, y_right, y_left, z_next)
    for device in partners:
        pl.semaphore_signal(barrier, inc=1, device_id=device, device_id_type=MESH)
    pl.semaphore_wait(barrier, len(partners))

    rows_over = [message(inputs[a].at[:, other], t_in.at[c, a], sibling) for a in (0, 1)]
    for copy in rows_over:
        copy.start()

    def block(a, slot, cols=mine):
        return xc.at[a, pl.ds(slot * BLOCK, BLOCK), cols]

    def hand_over(a, slot):
        copy = message(block(a, slot), block(a, slot), sibling)
        copy.start()
        return copy

    to_right, to_left, to_across, relay, over = {}, {}, {}, {}, {}
    for a in (0, 1):
        own_rows[a].wait()
        rows_over[a].wait_recv()

        @pl.loop(0, HALF // PANEL)
        def _(j, a=a):
            cols = pl.ds(pl.multiple_of(j * PANEL, PANEL), PANEL)
            both = jnp.concatenate([t_in[0, a, :, cols].astype(F32), t_in[1, a, :, cols].astype(F32)], axis=0)
            xc[a, 0:BLOCK, pl.ds(pl.multiple_of(c * HALF + j * PANEL, PANEL), PANEL)] = both.astype(BF16)

        to_right[a, OWN] = message(block(a, OWN), block(a, LEFT), x_right)
        to_left[a, OWN] = message(block(a, OWN), block(a, RIGHT), x_left)
        to_across[a, OWN] = message(block(a, OWN), block(a, ACROSS), z_across)
        for copy in (to_right[a, OWN], to_left[a, OWN], to_across[a, OWN]):
            copy.start()
        over[a, OWN] = hand_over(a, OWN)

    def relay_far(a):
        if a == 0:
            relay[a] = message(block(a, LEFT), block(a, FAR), x_right)
        else:
            relay[a] = message(block(a, RIGHT), block(a, FAR), x_left)
        relay[a].start()

    for a in (0, 1):
        first, second = (to_right, to_left) if a == 0 else (to_left, to_right)
        first[a, OWN].wait_recv()
        relay_far(a)
        over[a, LEFT if a == 0 else RIGHT] = hand_over(a, LEFT if a == 0 else RIGHT)
        to_across[a, OWN].wait_recv()
        to_right[a, ACROSS] = message(block(a, ACROSS), block(a, ACROSS_LEFT), x_right)
        to_left[a, ACROSS] = message(block(a, ACROSS), block(a, ACROSS_RIGHT), x_left)
        to_right[a, ACROSS].start()
        to_left[a, ACROSS].start()
        over[a, ACROSS] = hand_over(a, ACROSS)
        second[a, OWN].wait_recv()
        over[a, RIGHT if a == 0 else LEFT] = hand_over(a, RIGHT if a == 0 else LEFT)

    def gate_up(r0):
        gf[...] = jnp.zeros_like(gf)
        uf[...] = jnp.zeros_like(uf)

        @pl.loop(0, 4)
        def _(k):
            ks = pl.ds(pl.multiple_of(k * 1024, 1024), 1024)
            rows = xc[0, r0:r0 + PART, ks]
            gf[...] += mm(rows, wg[ks, :])
            uf[...] += mm(rows, wu[ks, :])

    def backward(r0):
        df[...] = jnp.zeros_like(df)

        @pl.loop(0, 4)
        def _(k):
            ks = pl.ds(pl.multiple_of(k * 1024, 1024), 1024)
            df[...] += mm_nt(xc[1, r0:r0 + PART, ks], wd[:, ks])

        @pl.loop(0, PART // 32)
        def _(i):
            r = pl.ds(pl.multiple_of(i * 32, 32), 32)
            w = pl.ds(pl.multiple_of(r0 + i * 32, 32), 32)
            gate, up, dhidden = gf[r, :], uf[r, :], df[r, :]
            s = 1.0 / (1.0 + jnp.exp(-gate))
            swish = gate * s
            hid[w, :] = (swish * up).astype(BF16)
            dg[w, :] = (dhidden * up * s * (1.0 + gate * (1.0 - s))).astype(BF16)
            du[w, :] = (dhidden * swish).astype(BF16)

    def transpose(q, src, start, stop):
        for i in range(start, stop):
            lt[q * PANEL:(q + 1) * PANEL, i * 128:(i + 1) * 128] = src[i * 128:(i + 1) * 128, :].T

    def wait_over(a, slots):
        for slot in slots:
            over[a, slot].wait_recv()

    weights[0].wait()
    weights[1].wait()
    wait_over(0, (OWN, LEFT, RIGHT, ACROSS))
    gate_up(0)
    weights[2].wait()
    wait_over(1, (OWN, LEFT, RIGHT, ACROSS))
    backward(0)
    for a in (0, 1):
        relay[a].wait_recv()
        to_across[a, FAR] = message(block(a, FAR), block(a, ACROSS_FAR), z_across)
        to_across[a, FAR].start()
        over[a, FAR] = hand_over(a, FAR)
    for q, src in enumerate((dg, du, hid)):
        transpose(q, src, 0, 2)
    for a in (0, 1):
        to_right[a, ACROSS].wait_recv()
        over[a, ACROSS_LEFT] = hand_over(a, ACROSS_LEFT)
        to_left[a, ACROSS].wait_recv()
        over[a, ACROSS_RIGHT] = hand_over(a, ACROSS_RIGHT)
        to_across[a, FAR].wait_recv()
        over[a, ACROSS_FAR] = hand_over(a, ACROSS_FAR)
        wait_over(a, (FAR, ACROSS_LEFT, ACROSS_RIGHT, ACROSS_FAR))
        if a == 0:
            gate_up(PART)
    backward(PART)
    gather = list(pending)

    def place(z, yr):
        d = ((zl + z) % 2) * 4 + (y + yr) % 4
        return pl.ds(pl.multiple_of(d * PANEL, PANEL), PANEL)

    def grad_gate_up(z, yr):
        @pl.loop(0, 2)
        def _(q):
            r = pl.ds(pl.multiple_of(q * PANEL, PANEL), PANEL)
            pgu[z, yr, r, :] = mm(lt[r, :], xc[0, :, place(z, yr)]).astype(BF16)

    def grad_down(z, yr):
        total = mm(lt[2 * PANEL:, :], xc[1, :, place(z, yr)]).astype(BF16)
        if z:
            pdo[yr] = total
        else:
            wd[:, yr * PANEL:(yr + 1) * PANEL] = total

    class Ring:
        def __init__(self, own, spare, right, left, rows, step):
            self.own, self.spare, self.right, self.left = own, spare, right, left
            self.rows, self.step = rows, step

        def far(self):
            own, spare = self.own, self.spare
            self.far0 = message(own(0, 2), spare(0, 0), self.right)
            self.far1 = message(own(1, 2), spare(0, 1), self.left)
            self.far0.start()
            self.far1.start()

        def near(self):
            own, spare = self.own, self.spare
            self.near1 = message(own(1, 1), spare(1, 1), self.right)
            self.near0 = message(own(0, 3), spare(1, 0), self.left)
            self.near1.start()
            self.near0.start()

        def pass_on(self):
            own, spare = self.own, self.spare
            self.far0.wait_recv()
            add_into(own(0, 1), spare(0, 0), self.rows, self.step)
            self.last0 = message(own(0, 1), spare(2, 0), self.right)
            self.last0.start()
            self.far1.wait_recv()
            add_into(own(1, 3), spare(0, 1), self.rows, self.step)
            self.last1 = message(own(1, 3), spare(2, 1), self.left)
            self.last1.start()

        def finish(self, lane, extra=()):
            (self.near0, self.near1)[lane].wait_recv()
            (self.last0, self.last1)[lane].wait_recv()
            spare = self.spare
            mine = self.own(lane, 0)
            sum_to(mine, (mine, spare(1, lane), spare(2, lane)) + tuple(extra), self.rows, self.step)

    def gate_up_ring(z):
        return Ring(
            lambda lane, yr: pgu.at[z, yr, pl.ds(lane * PANEL, PANEL), :],
            lambda kind, lane: gring.at[z, kind, lane],
            y_right, y_left, PANEL, 64,
        )

    down_ring = Ring(
        lambda lane, yr: wd.at[pl.ds(lane * 256, 256), pl.ds(yr * PANEL, PANEL)],
        lambda kind, lane: dring.at[kind, lane],
        y_right, y_left, 256, 64,
    )

    slot_of = ((OWN, RIGHT, FAR, LEFT), (ACROSS, ACROSS_RIGHT, ACROSS_FAR, ACROSS_LEFT))

    def token_rows(m, slot, cols):
        rows = pl.ds(slot * BLOCK, BLOCK)
        return am.at[rows, cols] if m == 0 else xc.at[1, rows, cols]

    def token_ring(m, z):
        return Ring(
            lambda lane, xr: token_rows(m, slot_of[z][xr], pl.ds(lane * LANE, LANE)),
            lambda kind, lane: mring.at[m, z, kind, lane],
            x_right, x_left, BLOCK, 16,
        )

    gu = [gate_up_ring(0), gate_up_ring(1)]
    tr = {(m, z): token_ring(m, z) for m in (0, 1) for z in (0, 1)}

    transpose(0, dg, 2, 5)
    transpose(1, du, 2, 5)
    grad_gate_up(1, 2)
    gu[1].far()
    transpose(2, hid, 2, 5)
    down_z = {}
    for yr in (2, 1, 3, 0):
        grad_down(1, yr)
        down_z[yr] = message(pdo.at[yr], dz.at[yr], z_next)
        down_z[yr].start()
    grad_gate_up(1, 1)
    grad_gate_up(1, 3)
    gu[1].near()

    @pl.loop(0, 4)
    def _(j):
        cols = pl.ds(pl.multiple_of((1 - c) * HALF + j * PANEL, PANEL), PANEL)
        pgu[0, j, 0:ROWS, :] = mm(hid[...], wd[:, cols]).astype(BF16)

    mixed_over = [message(pgu.at[0, j, pl.ds(0, ROWS), :], sm.at[j], sibling) for j in range(4)]
    for copy in mixed_over:
        copy.start()

    @pl.loop(0, 4)
    def _(j):
        cols = pl.ds(pl.multiple_of(c * HALF + j * PANEL, PANEL), PANEL)
        am[:, pl.ds(pl.multiple_of(j * PANEL, PANEL), PANEL)] = mm(hid[...], wd[:, cols]).astype(BF16)

    grad_gate_up(1, 0)
    for copy in mixed_over:
        wait_send(copy)
    grad_gate_up(0, 2)
    gu[0].far()
    grad_gate_up(0, 1)
    grad_gate_up(0, 3)
    gu[0].near()

    for j in range(4):
        mixed_over[j].wait_recv()
        add_into(am.at[:, pl.ds(j * PANEL, PANEL)], sm.at[j], ROWS, 64)
    pl.semaphore_signal(credit, inc=1, device_id=sibling, device_id_type=MESH)
    for z in (1, 0):
        tr[0, z].far()
        tr[0, z].near()
    gu[1].pass_on()
    for yr in (2, 1, 3, 0):
        grad_down(0, yr)

    for copy in gather:
        wait_send(copy)

    def input_grad(base, j):
        w = pl.ds(pl.multiple_of(base * HALF + j * PANEL, PANEL), PANEL)
        return (mm_nt(dg[...], wg[w, :]) + mm_nt(du[...], wu[w, :])).astype(BF16)

    @pl.loop(0, 4)
    def _(j):
        xc[1, :, pl.ds(pl.multiple_of(HALF + j * PANEL, PANEL), PANEL)] = input_grad(1 - c, j)

    pl.semaphore_wait(credit, 1)
    ig_over = [message(xc.at[1, :, pl.ds(HALF + j * PANEL, PANEL)], sm.at[j], sibling) for j in range(4)]
    for copy in ig_over:
        copy.start()

    @pl.loop(0, 4)
    def _(j):
        xc[1, :, pl.ds(pl.multiple_of(j * PANEL, PANEL), PANEL)] = input_grad(c, j)

    for j in range(4):
        ig_over[j].wait_recv()
        add_into(xc.at[1, :, pl.ds(j * PANEL, PANEL)], sm.at[j], ROWS, 64)
    for z in (1, 0):
        tr[1, z].far()
        tr[1, z].near()
    for z in (1, 0):
        tr[0, z].pass_on()
    grad_gate_up(0, 0)
    gu[0].pass_on()
    for z in (1, 0):
        tr[1, z].pass_on()

    token_z = {}

    def send_across(m):
        for lane in (0, 1):
            tr[m, 1].finish(lane)
        token_z[m] = message(token_rows(m, ACROSS, pl.ds(0, HALF)), mz.at[m], z_across)
        token_z[m].start()

    def down_step(yr):
        down_z[yr].wait_recv()
        add_into(wd.at[:, pl.ds(yr * PANEL, PANEL)], dz.at[yr], PANEL, 64)

    send_across(0)
    down_step(2)
    down_ring.far()
    gu_z = []
    for lane in (0, 1):
        gu[1].finish(lane)
        copy = message(pgu.at[1, 0, pl.ds(lane * PANEL, PANEL), :], gz.at[lane], z_next)
        copy.start()
        gu_z.append(copy)
    send_across(1)
    down_step(1)
    down_step(3)
    down_ring.near()
    down_step(0)
    down_ring.pass_on()

    outs = []
    for m, out in enumerate((mixed_out, ig_out)):
        for lane in (0, 1):
            tr[m, 0].finish(lane)
        token_z[m].wait_recv()
        rows = token_rows(m, OWN, pl.ds(0, HALF))

        @pl.loop(0, 4)
        def _(j, m=m, rows=rows):
            cols = pl.ds(pl.multiple_of(j * PANEL, PANEL), PANEL)
            total = rows[:, cols].astype(F32) + mz[m, :, cols].astype(F32)
            top, bottom = total[:BLOCK // 2], total[BLOCK // 2:]
            fo[m, 0, :, cols] = jnp.where(c == 0, top, bottom).astype(BF16)
            fo[m, 1, :, cols] = jnp.where(c == 0, bottom, top).astype(BF16)

        keep = pltpu.make_async_copy(fo.at[m, 0], out.at[:, mine], local_sem.at[5 + m])
        give = message(fo.at[m, 1], out.at[:, mine], sibling)
        keep.start()
        give.start()
        outs.append((keep, give))

    grads = []
    for lane, out in enumerate((gate_out, up_out)):
        gu_z[lane].wait_recv()
        gu[0].finish(lane, (gz.at[lane],))
        copy = pltpu.make_async_copy(pgu.at[0, 0, pl.ds(lane * PANEL, PANEL), :], out, local_sem.at[7 + lane])
        copy.start()
        grads.append(copy)
    for lane in (0, 1):
        down_ring.finish(lane)
    copy = pltpu.make_async_copy(wd.at[:, pl.ds(0, PANEL)], down_out, local_sem.at[9])
    copy.start()
    grads.append(copy)

    for keep, give in outs:
        keep.wait()
        give.wait_recv()
    for copy in grads:
        copy.wait()
    for copy in pending:
        wait_send(copy)


def on_device(tokens, w_gate, w_up, w_down, cotangent):
    v = lambda *shape: pltpu.VMEM(shape, BF16)
    mixed, input_grad, gate, up, down = pl.pallas_call(
        kernel,
        out_shape=[jax.ShapeDtypeStruct((BLOCK // 2, D), BF16)] * 2
        + [jax.ShapeDtypeStruct((PANEL, PANEL), BF16)] * 3,
        in_specs=[pl.BlockSpec(memory_space=pl.ANY)] * 5,
        out_specs=[pl.BlockSpec(memory_space=pl.ANY)] * 5,
        scratch_shapes=[
            v(D, PANEL), v(D, PANEL), v(PANEL, D),
            v(2, ROWS, D),
            v(ROWS, PANEL), v(ROWS, PANEL), v(ROWS, PANEL),
            v(3 * PANEL, ROWS),
            pltpu.VMEM((PART, PANEL), F32), pltpu.VMEM((PART, PANEL), F32), pltpu.VMEM((PART, PANEL), F32),
            v(ROWS, HALF), v(4, ROWS, PANEL),
            v(2, 4, 2 * PANEL, PANEL), v(4, PANEL, PANEL),
            v(2, 2, 3, 2, BLOCK, LANE), v(2, BLOCK, HALF),
            v(2, 3, 2, PANEL, PANEL), v(2, PANEL, PANEL),
            v(4, PANEL, PANEL), v(3, 2, PANEL // 2, PANEL),
            v(2, 2, BLOCK // 2, HALF), v(2, 2, BLOCK // 2, HALF),
            pltpu.SemaphoreType.DMA((MESSAGES,)),
            pltpu.SemaphoreType.DMA((MESSAGES,)),
            pltpu.SemaphoreType.DMA((10,)),
            pltpu.SemaphoreType.REGULAR,
        ],
        compiler_params=pltpu.CompilerParams(
            collective_id=0, has_side_effects=True, vmem_limit_bytes=63 * 1024 * 1024
        ),
        cost_estimate=pl.CostEstimate(flops=24_200_000_000, bytes_accessed=16_000_000, transcendentals=330_000),
    )(tokens, w_gate, w_up, w_down, cotangent)
    return mixed, input_grad, gate.T, up.T, down


def solution(mesh):
    in_specs = (
        P(("dp", "mp"), None),
        P(None, "mp"),
        P(None, "mp"),
        P("mp", None),
        P(("dp", "mp"), None),
    )
    out_specs = (
        P(("dp", "mp"), None),
        P(("dp", "mp"), None),
        P("dp", "mp"),
        P("dp", "mp"),
        P("mp", "dp"),
    )
    return jax.shard_map(
        on_device, mesh=mesh, in_specs=in_specs, out_specs=out_specs, check_vma=False
    )
```

```python
import jax
import jax.numpy as jnp
from jax import lax
from jax.experimental import pallas as pl
from jax.experimental.pallas import tpu as pltpu
from jax.sharding import PartitionSpec as P

MESH = pl.DeviceIdType.MESH
BF16 = jnp.bfloat16
F32 = jnp.float32
D = 4096
HALF = D // 2
LANE = HALF // 2
PANEL = 512
ROWS = 640
BLOCK = 80
PART = 320
MESSAGES = 110

OWN, LEFT, RIGHT, ACROSS, FAR, ACROSS_LEFT, ACROSS_RIGHT, ACROSS_FAR = range(8)


def mm(a, b):
    return jnp.dot(a, b, preferred_element_type=F32)


def mm_nt(a, b):
    return lax.dot_general(a, b, (((1,), (1,)), ((), ())), preferred_element_type=F32)


def add_into(dst, src, rows, step):
    @pl.loop(0, rows // step)
    def _(i):
        r = pl.ds(pl.multiple_of(i * step, step), step)
        dst[r, :] = (dst[r, :].astype(F32) + src[r, :].astype(F32)).astype(BF16)


def sum_to(dst, terms, rows, step):
    @pl.loop(0, rows // step)
    def _(i):
        r = pl.ds(pl.multiple_of(i * step, step), step)
        total = terms[0][r, :].astype(F32)
        for term in terms[1:]:
            total += term[r, :].astype(F32)
        dst[r, :] = total.astype(BF16)


def kernel(
    tok_hbm, wg_hbm, wu_hbm, wd_hbm, cot_hbm,
    mixed_out, ig_out, gate_out, up_out, down_out,
    wg, wu, wd, xc, hid, dg, du, lt, gf, uf, df, am, sm, pgu, pdo,
    mring, mz, gring, gz, dz, dring, t_in, fo,
    send_sem, recv_sem, local_sem, credit,
):
    dp, mp = lax.axis_index("dp"), lax.axis_index("mp")
    zl, y = dp // 4, dp % 4
    zh, x, c = mp // 8, (mp // 2) % 4, mp % 2
    x_right = (dp, zh * 8 + ((x + 1) % 4) * 2 + c)
    x_left = (dp, zh * 8 + ((x + 3) % 4) * 2 + c)
    z_across = (dp, (1 - zh) * 8 + x * 2 + c)
    sibling = (dp, zh * 8 + x * 2 + (1 - c))
    y_right = (zl * 4 + (y + 1) % 4, mp)
    y_left = (zl * 4 + (y + 3) % 4, mp)
    z_next = ((1 - zl) * 4 + y, mp)
    mine = pl.ds(pl.multiple_of(c * HALF, HALF), HALF)
    other = pl.ds(pl.multiple_of((1 - c) * HALF, HALF), HALF)

    pending = []

    def message(src, dst, device):
        n = len(pending)
        copy = pltpu.make_async_remote_copy(
            src_ref=src, dst_ref=dst, send_sem=send_sem.at[n], recv_sem=recv_sem.at[n],
            device_id=device, device_id_type=MESH,
        )
        pending.append(copy)
        return copy

    sent = set()

    def wait_send(copy):
        if id(copy) not in sent:
            sent.add(id(copy))
            copy.wait_send()

    weights = [
        pltpu.make_async_copy(src, dst, local_sem.at[n])
        for n, (src, dst) in enumerate(((wg_hbm, wg), (wu_hbm, wu), (wd_hbm, wd)))
    ]
    inputs = (tok_hbm, cot_hbm)
    own_rows = [pltpu.make_async_copy(inputs[a].at[:, mine], t_in.at[c, a], local_sem.at[3 + a]) for a in (0, 1)]
    for copy in own_rows:
        copy.start()

    barrier = pltpu.get_barrier_semaphore()
    partners = (x_right, x_left, z_across, sibling, y_right, y_left, z_next)
    for device in partners:
        pl.semaphore_signal(barrier, inc=1, device_id=device, device_id_type=MESH)
    pl.semaphore_wait(barrier, len(partners))

    rows_over = [message(inputs[a].at[:, other], t_in.at[c, a], sibling) for a in (0, 1)]
    for copy in rows_over:
        copy.start()

    def block(a, slot, cols=mine):
        return xc.at[a, pl.ds(slot * BLOCK, BLOCK), cols]

    def hand_over(a, slot):
        copy = message(block(a, slot), block(a, slot), sibling)
        copy.start()
        return copy

    parts = [pl.ds(pl.multiple_of(c * HALF + i * LANE, LANE), LANE) for i in (0, 1)]
    to_right, to_left, to_across, relay, over = {}, {}, {}, {}, {}
    for a in (0, 1):
        own_rows[a].wait()
        rows_over[a].wait_recv()

        @pl.loop(0, HALF // PANEL)
        def _(j, a=a):
            cols = pl.ds(pl.multiple_of(j * PANEL, PANEL), PANEL)
            both = jnp.concatenate([t_in[0, a, :, cols].astype(F32), t_in[1, a, :, cols].astype(F32)], axis=0)
            xc[a, 0:BLOCK, pl.ds(pl.multiple_of(c * HALF + j * PANEL, PANEL), PANEL)] = both.astype(BF16)

        to_across[a, OWN] = message(block(a, OWN), block(a, ACROSS), z_across)
        if a == 0:
            to_right[0, OWN] = message(block(0, OWN), block(0, LEFT), x_right)
            to_right[0, OWN].start()
        else:
            to_left[1, OWN] = message(block(1, OWN), block(1, RIGHT), x_left)
            to_left[1, OWN].start()
            to_right[1, OWN] = [message(block(1, OWN, cols), block(1, LEFT, cols), x_right) for cols in parts]
            to_left[0, OWN] = [message(block(0, OWN, cols), block(0, RIGHT, cols), x_left) for cols in parts]
            to_right[1, OWN][0].start()
            to_left[0, OWN][0].start()
        to_across[a, OWN].start()
        over[a, OWN] = hand_over(a, OWN)
    for copy in weights:
        copy.start()

    def relay_far(a):
        if a == 0:
            relay[a] = message(block(a, LEFT), block(a, FAR), x_right)
        else:
            relay[a] = message(block(a, RIGHT), block(a, FAR), x_left)
        relay[a].start()

    def from_across(a):
        to_across[a, OWN].wait_recv()
        to_right[a, ACROSS] = message(block(a, ACROSS), block(a, ACROSS_LEFT), x_right)
        to_left[a, ACROSS] = message(block(a, ACROSS), block(a, ACROSS_RIGHT), x_left)
        to_right[a, ACROSS].start()
        to_left[a, ACROSS].start()
        over[a, ACROSS] = hand_over(a, ACROSS)

    def from_far(a):
        relay[a].wait_recv()
        to_across[a, FAR] = message(block(a, FAR), block(a, ACROSS_FAR), z_across)
        to_across[a, FAR].start()
        over[a, FAR] = hand_over(a, FAR)

    def arrived(copy, a, slot):
        copy.wait_recv()
        over[a, slot] = hand_over(a, slot)

    def wait_over(a, slots):
        for slot in slots:
            over[a, slot].wait_recv()

    def columns(k):
        return pl.ds(pl.multiple_of((c * 2 + k) % 4 * 1024, 1024), 1024)

    def gate_up(r0, slots):
        gf[...] = jnp.zeros_like(gf)
        uf[...] = jnp.zeros_like(uf)

        def step(k):
            ks = columns(k)
            rows = xc[0, r0:r0 + PART, ks]
            gf[...] += mm(rows, wg[ks, :])
            uf[...] += mm(rows, wu[ks, :])

        pl.loop(0, 2)(step)
        wait_over(0, slots)
        pl.loop(2, 4)(step)

        @pl.loop(0, PART // 32)
        def _(i):
            r = pl.ds(pl.multiple_of(i * 32, 32), 32)
            w = pl.ds(pl.multiple_of(r0 + i * 32, 32), 32)
            gate, up = gf[r, :], uf[r, :]
            s = 1.0 / (1.0 + jnp.exp(-gate))
            swish = gate * s
            hid[w, :] = (swish * up).astype(BF16)
            gf[r, :] = up * s * (1.0 + gate * (1.0 - s))
            uf[r, :] = swish

    def backward(r0, slots):
        df[...] = jnp.zeros_like(df)

        def step(k):
            ks = columns(k)
            df[...] += mm_nt(xc[1, r0:r0 + PART, ks], wd[:, ks])

        pl.loop(0, 2)(step)
        wait_over(1, slots)
        pl.loop(2, 4)(step)

        @pl.loop(0, PART // 32)
        def _(i):
            r = pl.ds(pl.multiple_of(i * 32, 32), 32)
            w = pl.ds(pl.multiple_of(r0 + i * 32, 32), 32)
            dhidden = df[r, :]
            dg[w, :] = (dhidden * gf[r, :]).astype(BF16)
            du[w, :] = (dhidden * uf[r, :]).astype(BF16)

    def mixed_part(r0):
        @pl.loop(0, 4)
        def _(j):
            cols = pl.ds(pl.multiple_of((1 - c) * HALF + j * PANEL, PANEL), PANEL)
            pgu[0, j, r0:r0 + PART, :] = mm(hid[r0:r0 + PART, :], wd[:, cols]).astype(BF16)

        @pl.loop(0, 4)
        def _(j):
            cols = pl.ds(pl.multiple_of(c * HALF + j * PANEL, PANEL), PANEL)
            total = mm(hid[r0:r0 + PART, :], wd[:, cols]).astype(BF16)
            am[r0:r0 + PART, pl.ds(pl.multiple_of(j * PANEL, PANEL), PANEL)] = total

    def transpose(q, src, start, stop):
        for i in range(start, stop):
            lt[q * PANEL:(q + 1) * PANEL, i * 128:(i + 1) * 128] = src[i * 128:(i + 1) * 128, :].T

    to_right[0, OWN].wait_recv()
    relay_far(0)
    to_right[1, OWN][1].start()
    to_left[1, OWN].wait_recv()
    relay_far(1)
    to_left[0, OWN][1].start()
    over[0, LEFT] = hand_over(0, LEFT)
    over[1, RIGHT] = hand_over(1, RIGHT)
    from_across(0)
    from_across(1)
    from_far(0)
    from_far(1)
    for a, slot, halves in ((0, RIGHT, to_left[0, OWN]), (1, LEFT, to_right[1, OWN])):
        halves[0].wait_recv()
        arrived(halves[1], a, slot)
    near = (OWN, LEFT, RIGHT, ACROSS)
    distant = (FAR, ACROSS_LEFT, ACROSS_RIGHT, ACROSS_FAR)
    weights[0].wait()
    weights[1].wait()
    gate_up(0, near)
    weights[2].wait()
    backward(0, near)
    for q, src in enumerate((dg, du, hid)):
        transpose(q, src, 0, 2)
    mixed_part(0)
    for a in (0, 1):
        arrived(to_left[a, ACROSS], a, ACROSS_RIGHT)
        arrived(to_right[a, ACROSS], a, ACROSS_LEFT)
        arrived(to_across[a, FAR], a, ACROSS_FAR)
        if a == 0:
            gate_up(PART, distant)
            transpose(2, hid, 2, 5)
    backward(PART, distant)
    gather = list(pending)

    def place(z, yr):
        d = ((zl + z) % 2) * 4 + (y + yr) % 4
        return pl.ds(pl.multiple_of(d * PANEL, PANEL), PANEL)

    def grad_lane(z, yr, lane):
        r = pl.ds(pl.multiple_of(lane * PANEL, PANEL), PANEL)
        pgu[z, yr, r, :] = mm(lt[r, :], xc[0, :, place(z, yr)]).astype(BF16)

    def grad_gate_up(z, yr):
        @pl.loop(0, 2)
        def _(q):
            grad_lane(z, yr, q)

    def grad_down(z, yr):
        total = mm(lt[2 * PANEL:, :], xc[1, :, place(z, yr)]).astype(BF16)
        if z:
            pdo[yr] = total
        else:
            wd[:, yr * PANEL:(yr + 1) * PANEL] = total

    class Ring:
        def __init__(self, own, spare, right, left, rows, step):
            self.own, self.spare, self.right, self.left = own, spare, right, left
            self.rows, self.step = rows, step

        def far_lane(self, lane):
            copy = message(self.own(lane, 2), self.spare(0, lane), (self.right, self.left)[lane])
            setattr(self, ("far0", "far1")[lane], copy)
            copy.start()

        def far(self):
            self.far_lane(0)
            self.far_lane(1)

        def near(self):
            own, spare = self.own, self.spare
            self.near1 = message(own(1, 1), spare(1, 1), self.right)
            self.near0 = message(own(0, 3), spare(1, 0), self.left)
            self.near1.start()
            self.near0.start()

        def pass_on(self):
            own, spare = self.own, self.spare
            self.far0.wait_recv()
            add_into(own(0, 1), spare(0, 0), self.rows, self.step)
            self.last0 = message(own(0, 1), spare(2, 0), self.right)
            self.last0.start()
            self.far1.wait_recv()
            add_into(own(1, 3), spare(0, 1), self.rows, self.step)
            self.last1 = message(own(1, 3), spare(2, 1), self.left)
            self.last1.start()

        def finish(self, lane, extra=()):
            (self.near0, self.near1)[lane].wait_recv()
            (self.last0, self.last1)[lane].wait_recv()
            spare = self.spare
            mine = self.own(lane, 0)
            sum_to(mine, (mine, spare(1, lane), spare(2, lane)) + tuple(extra), self.rows, self.step)

    def gate_up_ring(z):
        return Ring(
            lambda lane, yr: pgu.at[z, yr, pl.ds(lane * PANEL, PANEL), :],
            lambda kind, lane: gring.at[z, kind, lane],
            y_right, y_left, PANEL, 64,
        )

    down_ring = Ring(
        lambda lane, yr: wd.at[pl.ds(lane * 256, 256), pl.ds(yr * PANEL, PANEL)],
        lambda kind, lane: dring.at[kind, lane],
        y_right, y_left, 256, 64,
    )

    slot_of = ((OWN, RIGHT, FAR, LEFT), (ACROSS, ACROSS_RIGHT, ACROSS_FAR, ACROSS_LEFT))

    def token_rows(m, slot, cols):
        rows = pl.ds(slot * BLOCK, BLOCK)
        return am.at[rows, cols] if m == 0 else xc.at[1, rows, cols]

    def token_ring(m, z):
        return Ring(
            lambda lane, xr: token_rows(m, slot_of[z][xr], pl.ds(lane * LANE, LANE)),
            lambda kind, lane: mring.at[m, z, kind, lane],
            x_right, x_left, BLOCK, 16,
        )

    gu = [gate_up_ring(0), gate_up_ring(1)]
    tr = {(m, z): token_ring(m, z) for m in (0, 1) for z in (0, 1)}

    transpose(0, dg, 2, 5)
    grad_lane(1, 2, 0)
    gu[1].far_lane(0)
    transpose(1, du, 2, 5)
    grad_lane(1, 2, 1)
    gu[1].far_lane(1)
    down_z = {}
    for yr in (2, 1, 3, 0):
        grad_down(1, yr)
        down_z[yr] = message(pdo.at[yr], dz.at[yr], z_next)
        down_z[yr].start()
    grad_gate_up(1, 1)
    grad_gate_up(1, 3)
    gu[1].near()
    mixed_part(PART)
    mixed_over = [message(pgu.at[0, j, pl.ds(0, ROWS), :], sm.at[j], sibling) for j in range(4)]
    for copy in mixed_over:
        copy.start()
    for yr in (2, 1, 3, 0):
        grad_down(0, yr)
    for j in range(4):
        mixed_over[j].wait_recv()
        add_into(am.at[:, pl.ds(j * PANEL, PANEL)], sm.at[j], ROWS, 64)
    pl.semaphore_signal(credit, inc=1, device_id=sibling, device_id_type=MESH)
    tr[0, 1].far()
    tr[0, 1].near()
    for copy in mixed_over:
        wait_send(copy)
    grad_gate_up(0, 2)
    gu[0].far()
    grad_gate_up(0, 1)
    grad_gate_up(0, 3)
    gu[0].near()

    for copy in gather:
        wait_send(copy)

    def input_grad(base, j):
        w = pl.ds(pl.multiple_of(base * HALF + j * PANEL, PANEL), PANEL)
        return (mm_nt(dg[...], wg[w, :]) + mm_nt(du[...], wu[w, :])).astype(BF16)

    @pl.loop(0, 4)
    def _(j):
        xc[1, :, pl.ds(pl.multiple_of(HALF + j * PANEL, PANEL), PANEL)] = input_grad(1 - c, j)

    pl.semaphore_wait(credit, 1)
    ig_over = [message(xc.at[1, :, pl.ds(HALF + j * PANEL, PANEL)], sm.at[j], sibling) for j in range(4)]
    for copy in ig_over:
        copy.start()

    @pl.loop(0, 4)
    def _(j):
        xc[1, :, pl.ds(pl.multiple_of(j * PANEL, PANEL), PANEL)] = input_grad(c, j)

    tr[0, 1].pass_on()
    for j in range(4):
        ig_over[j].wait_recv()
        add_into(xc.at[1, :, pl.ds(j * PANEL, PANEL)], sm.at[j], ROWS, 64)
    tr[1, 1].far()
    tr[1, 1].near()
    for m in (0, 1):
        tr[m, 0].far()
        tr[m, 0].near()
    gu[1].pass_on()
    grad_gate_up(1, 0)
    grad_gate_up(0, 0)

    token_z = {}

    def send_across(m):
        for lane in (0, 1):
            tr[m, 1].finish(lane)
        token_z[m] = message(token_rows(m, ACROSS, pl.ds(0, HALF)), mz.at[m], z_across)
        token_z[m].start()

    def down_step(yr):
        down_z[yr].wait_recv()
        add_into(wd.at[:, pl.ds(yr * PANEL, PANEL)], dz.at[yr], PANEL, 64)

    down_step(2)
    down_ring.far()
    send_across(0)
    tr[1, 1].pass_on()
    down_step(1)
    down_step(3)
    down_ring.near()
    gu[0].pass_on()
    send_across(1)
    for m in (0, 1):
        tr[m, 0].pass_on()
    down_step(0)
    gu_z = []
    for lane in (0, 1):
        gu[1].finish(lane)
        copy = message(pgu.at[1, 0, pl.ds(lane * PANEL, PANEL), :], gz.at[lane], z_next)
        copy.start()
        gu_z.append(copy)
    down_ring.pass_on()

    outs = []
    for m, out in enumerate((mixed_out, ig_out)):
        for lane in (0, 1):
            tr[m, 0].finish(lane)
        token_z[m].wait_recv()
        rows = token_rows(m, OWN, pl.ds(0, HALF))

        @pl.loop(0, 4)
        def _(j, m=m, rows=rows):
            cols = pl.ds(pl.multiple_of(j * PANEL, PANEL), PANEL)
            total = rows[:, cols].astype(F32) + mz[m, :, cols].astype(F32)
            top, bottom = total[:BLOCK // 2], total[BLOCK // 2:]
            fo[m, 0, :, cols] = jnp.where(c == 0, top, bottom).astype(BF16)
            fo[m, 1, :, cols] = jnp.where(c == 0, bottom, top).astype(BF16)

        keep = pltpu.make_async_copy(fo.at[m, 0], out.at[:, mine], local_sem.at[5 + m])
        give = message(fo.at[m, 1], out.at[:, mine], sibling)
        keep.start()
        give.start()
        outs.append((keep, give))

    grads = []
    for lane, out in enumerate((gate_out, up_out)):
        gu_z[lane].wait_recv()
        gu[0].finish(lane, (gz.at[lane],))
        gring[0, 0, lane] = pgu[0, 0, lane * PANEL:(lane + 1) * PANEL, :].T
        copy = pltpu.make_async_copy(gring.at[0, 0, lane], out, local_sem.at[7 + lane])
        copy.start()
        grads.append(copy)
    for lane in (0, 1):
        down_ring.finish(lane)
    copy = pltpu.make_async_copy(wd.at[:, pl.ds(0, PANEL)], down_out, local_sem.at[9])
    copy.start()
    grads.append(copy)

    for keep, give in outs:
        keep.wait()
        give.wait_recv()
    for copy in grads:
        copy.wait()
    for copy in pending:
        wait_send(copy)


def arrange(*refs):
    sources, results, held, sem = refs[:5], refs[5:10], refs[10:15], refs[15]
    ins = [pltpu.make_async_copy(sources[n], held[n], sem.at[n]) for n in range(5)]
    outs = [pltpu.make_async_copy(held[n], results[n], sem.at[5 + n]) for n in range(5)]
    for copy in ins:
        copy.start()
    for n in range(5):
        ins[n].wait()
        outs[n].start()
    for copy in outs:
        copy.wait()


def on_device(tokens, w_gate, w_up, w_down, cotangent):
    v = lambda *shape: pltpu.VMEM(shape, BF16)
    shapes = [jax.ShapeDtypeStruct((BLOCK // 2, D), BF16)] * 2 + [jax.ShapeDtypeStruct((PANEL, PANEL), BF16)] * 3
    results = pl.pallas_call(
        kernel,
        out_shape=shapes,
        in_specs=[pl.BlockSpec(memory_space=pl.ANY)] * 5,
        out_specs=[pl.BlockSpec(memory_space=pl.ANY)] * 5,
        scratch_shapes=[
            v(D, PANEL), v(D, PANEL), v(PANEL, D),
            v(2, ROWS, D),
            v(ROWS, PANEL), v(ROWS, PANEL), v(ROWS, PANEL),
            v(3 * PANEL, ROWS),
            pltpu.VMEM((PART, PANEL), F32), pltpu.VMEM((PART, PANEL), F32), pltpu.VMEM((PART, PANEL), F32),
            v(ROWS, HALF), v(4, ROWS, PANEL),
            v(2, 4, 2 * PANEL, PANEL), v(4, PANEL, PANEL),
            v(2, 2, 3, 2, BLOCK, LANE), v(2, BLOCK, HALF),
            v(2, 3, 2, PANEL, PANEL), v(2, PANEL, PANEL),
            v(4, PANEL, PANEL), v(3, 2, PANEL // 2, PANEL),
            v(2, 2, BLOCK // 2, HALF), v(2, 2, BLOCK // 2, HALF),
            pltpu.SemaphoreType.DMA((MESSAGES,)),
            pltpu.SemaphoreType.DMA((MESSAGES,)),
            pltpu.SemaphoreType.DMA((10,)),
            pltpu.SemaphoreType.REGULAR,
        ],
        compiler_params=pltpu.CompilerParams(
            collective_id=0, has_side_effects=True, vmem_limit_bytes=63 * 1024 * 1024
        ),
        cost_estimate=pl.CostEstimate(flops=24_200_000_000, bytes_accessed=16_000_000, transcendentals=330_000),
    )(tokens, w_gate, w_up, w_down, cotangent)
    return pl.pallas_call(
        arrange,
        out_shape=shapes,
        in_specs=[pl.BlockSpec(memory_space=pl.ANY)] * 5,
        out_specs=[pl.BlockSpec(memory_space=pl.ANY)] * 5,
        scratch_shapes=[pltpu.VMEM(shape.shape, BF16) for shape in shapes] + [pltpu.SemaphoreType.DMA((10,))],
        compiler_params=pltpu.CompilerParams(vmem_limit_bytes=60 * 1024 * 1024),
    )(*results)


def solution(mesh):
    in_specs = (
        P(("dp", "mp"), None),
        P(None, "mp"),
        P(None, "mp"),
        P("mp", None),
        P(("dp", "mp"), None),
    )
    out_specs = (
        P(("dp", "mp"), None),
        P(("dp", "mp"), None),
        P("dp", "mp"),
        P("dp", "mp"),
        P("mp", "dp"),
    )
    return jax.shard_map(
        on_device, mesh=mesh, in_specs=in_specs, out_specs=out_specs, check_vma=False
    )
```

```python
import jax
import jax.numpy as jnp
from jax import lax
from jax.experimental import pallas as pl
from jax.experimental.pallas import tpu as pltpu
from jax.sharding import PartitionSpec as P

MESH = pl.DeviceIdType.MESH
BF16 = jnp.bfloat16
F32 = jnp.float32
D = 4096
HALF = D // 2
LANE = HALF // 2
PANEL = 512
ROWS = 640
BLOCK = 80
PART = 320
MESSAGES = 160
QROWS = PANEL // 2

OWN, LEFT, RIGHT, ACROSS, FAR, ACROSS_LEFT, ACROSS_RIGHT, ACROSS_FAR = range(8)


def mm(a, b):
    return jnp.dot(a, b, preferred_element_type=F32)


def mm_nt(a, b):
    return lax.dot_general(a, b, (((1,), (1,)), ((), ())), preferred_element_type=F32)


def add_into(dst, src, rows, step):
    @pl.loop(0, rows // step)
    def _(i):
        r = pl.ds(pl.multiple_of(i * step, step), step)
        dst[r, :] = (dst[r, :].astype(F32) + src[r, :].astype(F32)).astype(BF16)


def sum_to(dst, terms, rows, step):
    @pl.loop(0, rows // step)
    def _(i):
        r = pl.ds(pl.multiple_of(i * step, step), step)
        total = terms[0][r, :].astype(F32)
        for term in terms[1:]:
            total += term[r, :].astype(F32)
        dst[r, :] = total.astype(BF16)


def kernel(
    tok_hbm, wg_hbm, wu_hbm, wd_hbm, cot_hbm,
    mixed_out, ig_out, gate_out, up_out, down_out,
    wg, wu, wd, xc, hid, dg, du, lt, gf, uf, df, am, mb, sm, pdo,
    mring, mz, ry, lty, acc, gzs, gz, fin, dz, dbz, dring, t_in, fo,
    send_sem, recv_sem, local_sem, credit,
):
    dp, mp = lax.axis_index("dp"), lax.axis_index("mp")
    zl, y = dp // 4, dp % 4
    zh, x, c = mp // 8, (mp // 2) % 4, mp % 2
    x_right = (dp, zh * 8 + ((x + 1) % 4) * 2 + c)
    x_left = (dp, zh * 8 + ((x + 3) % 4) * 2 + c)
    z_across = (dp, (1 - zh) * 8 + x * 2 + c)
    sibling = (dp, zh * 8 + x * 2 + (1 - c))
    y_right = (zl * 4 + (y + 1) % 4, mp)
    y_left = (zl * 4 + (y + 3) % 4, mp)
    y_far = (zl * 4 + (y + 2) % 4, mp)
    z_next = ((1 - zl) * 4 + y, mp)
    mine = pl.ds(pl.multiple_of(c * HALF, HALF), HALF)
    other = pl.ds(pl.multiple_of((1 - c) * HALF, HALF), HALF)

    pending = []

    def message(src, dst, device):
        n = len(pending)
        copy = pltpu.make_async_remote_copy(
            src_ref=src, dst_ref=dst, send_sem=send_sem.at[n], recv_sem=recv_sem.at[n],
            device_id=device, device_id_type=MESH,
        )
        pending.append(copy)
        return copy

    sent = set()

    def wait_send(copy):
        if id(copy) not in sent:
            sent.add(id(copy))
            copy.wait_send()

    weights = [
        pltpu.make_async_copy(src, dst, local_sem.at[n])
        for n, (src, dst) in enumerate(((wg_hbm, wg), (wu_hbm, wu), (wd_hbm, wd)))
    ]
    inputs = (tok_hbm, cot_hbm)
    own_rows = [pltpu.make_async_copy(inputs[a].at[:, mine], t_in.at[c, a], local_sem.at[3 + a]) for a in (0, 1)]
    for copy in own_rows:
        copy.start()

    barrier = pltpu.get_barrier_semaphore()
    partners = (x_right, x_left, z_across, sibling, y_right, y_left, y_far, z_next)
    for device in partners:
        pl.semaphore_signal(barrier, inc=1, device_id=device, device_id_type=MESH)
    pl.semaphore_wait(barrier, len(partners))

    rows_over = [message(inputs[a].at[:, other], t_in.at[c, a], sibling) for a in (0, 1)]
    for copy in rows_over:
        copy.start()

    def block(a, slot, cols=mine):
        return xc.at[a, pl.ds(slot * BLOCK, BLOCK), cols]

    r_half = pl.ds(pl.multiple_of(c * PANEL, PANEL), PANEL)
    r_sent = {}

    def send_columns(slot):
        rows = pl.ds(slot * BLOCK, BLOCK)
        for yr, device in ((1, y_right), (3, y_left), (2, y_far)):
            cols = pl.ds(pl.multiple_of(c * HALF + (y + yr) % 4 * PANEL, PANEL), PANEL)
            r_sent[yr, slot] = message(xc.at[0, rows, cols], ry.at[3 - yr, rows, r_half], device)
            r_sent[yr, slot].start()

    def hand_over(a, slot):
        copy = message(block(a, slot), block(a, slot), sibling)
        copy.start()
        if a == 0:
            send_columns(slot)
        return copy

    parts = [pl.ds(pl.multiple_of(c * HALF + i * LANE, LANE), LANE) for i in (0, 1)]
    to_right, to_left, to_across, relay, over = {}, {}, {}, {}, {}
    for a in (0, 1):
        own_rows[a].wait()
        rows_over[a].wait_recv()

        @pl.loop(0, HALF // PANEL)
        def _(j, a=a):
            cols = pl.ds(pl.multiple_of(j * PANEL, PANEL), PANEL)
            both = jnp.concatenate([t_in[0, a, :, cols].astype(F32), t_in[1, a, :, cols].astype(F32)], axis=0)
            xc[a, 0:BLOCK, pl.ds(pl.multiple_of(c * HALF + j * PANEL, PANEL), PANEL)] = both.astype(BF16)

        to_across[a, OWN] = message(block(a, OWN), block(a, ACROSS), z_across)
        if a == 0:
            to_right[0, OWN] = message(block(0, OWN), block(0, LEFT), x_right)
            to_right[0, OWN].start()
        else:
            to_left[1, OWN] = message(block(1, OWN), block(1, RIGHT), x_left)
            to_left[1, OWN].start()
            to_right[1, OWN] = [message(block(1, OWN, cols), block(1, LEFT, cols), x_right) for cols in parts]
            to_left[0, OWN] = [message(block(0, OWN, cols), block(0, RIGHT, cols), x_left) for cols in parts]
            to_right[1, OWN][0].start()
            to_left[0, OWN][0].start()
        to_across[a, OWN].start()
        over[a, OWN] = hand_over(a, OWN)
    for copy in weights:
        copy.start()

    def relay_far(a):
        if a == 0:
            relay[a] = message(block(a, LEFT), block(a, FAR), x_right)
        else:
            relay[a] = message(block(a, RIGHT), block(a, FAR), x_left)
        relay[a].start()

    def from_across(a):
        to_across[a, OWN].wait_recv()
        to_right[a, ACROSS] = message(block(a, ACROSS), block(a, ACROSS_LEFT), x_right)
        to_left[a, ACROSS] = message(block(a, ACROSS), block(a, ACROSS_RIGHT), x_left)
        to_right[a, ACROSS].start()
        to_left[a, ACROSS].start()
        over[a, ACROSS] = hand_over(a, ACROSS)

    def from_far(a):
        relay[a].wait_recv()
        to_across[a, FAR] = message(block(a, FAR), block(a, ACROSS_FAR), z_across)
        to_across[a, FAR].start()
        over[a, FAR] = hand_over(a, FAR)

    def arrived(copy, a, slot):
        copy.wait_recv()
        over[a, slot] = hand_over(a, slot)

    def wait_over(a, slots):
        for slot in slots:
            over[a, slot].wait_recv()

    def columns(k):
        return pl.ds(pl.multiple_of((c * 2 + k) % 4 * 1024, 1024), 1024)

    def gate_up(r0, slots):
        gf[...] = jnp.zeros_like(gf)
        uf[...] = jnp.zeros_like(uf)

        def step(k):
            ks = columns(k)
            rows = xc[0, r0:r0 + PART, ks]
            gf[...] += mm(rows, wg[ks, :])
            uf[...] += mm(rows, wu[ks, :])

        pl.loop(0, 2)(step)
        wait_over(0, slots)
        pl.loop(2, 4)(step)

        @pl.loop(0, PART // 32)
        def _(i):
            r = pl.ds(pl.multiple_of(i * 32, 32), 32)
            w = pl.ds(pl.multiple_of(r0 + i * 32, 32), 32)
            gate, up = gf[r, :], uf[r, :]
            s = 1.0 / (1.0 + jnp.exp(-gate))
            swish = gate * s
            hid[w, :] = (swish * up).astype(BF16)
            gf[r, :] = up * s * (1.0 + gate * (1.0 - s))
            uf[r, :] = swish

    def backward(r0, slots):
        df[...] = jnp.zeros_like(df)

        def step(k):
            ks = columns(k)
            df[...] += mm_nt(xc[1, r0:r0 + PART, ks], wd[:, ks])

        pl.loop(0, 2)(step)
        wait_over(1, slots)
        pl.loop(2, 4)(step)

        @pl.loop(0, PART // 32)
        def _(i):
            r = pl.ds(pl.multiple_of(i * 32, 32), 32)
            w = pl.ds(pl.multiple_of(r0 + i * 32, 32), 32)
            dhidden = df[r, :]
            dg[w, :] = (dhidden * gf[r, :]).astype(BF16)
            du[w, :] = (dhidden * uf[r, :]).astype(BF16)

    def mixed_part(r0):
        @pl.loop(0, 4)
        def _(j):
            cols = pl.ds(pl.multiple_of((1 - c) * HALF + j * PANEL, PANEL), PANEL)
            mb[j, r0:r0 + PART, :] = mm(hid[r0:r0 + PART, :], wd[:, cols]).astype(BF16)

        @pl.loop(0, 4)
        def _(j):
            cols = pl.ds(pl.multiple_of(c * HALF + j * PANEL, PANEL), PANEL)
            total = mm(hid[r0:r0 + PART, :], wd[:, cols]).astype(BF16)
            am[r0:r0 + PART, pl.ds(pl.multiple_of(j * PANEL, PANEL), PANEL)] = total

    def transpose(q, src, start, stop):
        for i in range(start, stop):
            lt[q * PANEL:(q + 1) * PANEL, i * 128:(i + 1) * 128] = src[i * 128:(i + 1) * 128, :].T

    to_right[0, OWN].wait_recv()
    relay_far(0)
    to_right[1, OWN][1].start()
    to_left[1, OWN].wait_recv()
    relay_far(1)
    to_left[0, OWN][1].start()
    over[0, LEFT] = hand_over(0, LEFT)
    over[1, RIGHT] = hand_over(1, RIGHT)
    from_across(0)
    from_across(1)
    from_far(0)
    from_far(1)
    for a, slot, halves in ((0, RIGHT, to_left[0, OWN]), (1, LEFT, to_right[1, OWN])):
        halves[0].wait_recv()
        arrived(halves[1], a, slot)
    near = (OWN, LEFT, RIGHT, ACROSS)
    distant = (FAR, ACROSS_LEFT, ACROSS_RIGHT, ACROSS_FAR)
    weights[0].wait()
    weights[1].wait()
    gate_up(0, near)
    weights[2].wait()
    backward(0, near)
    for q, src in enumerate((dg, du, hid)):
        transpose(q, src, 0, 2)
    for a in (0, 1):
        arrived(to_left[a, ACROSS], a, ACROSS_RIGHT)
        arrived(to_right[a, ACROSS], a, ACROSS_LEFT)
        arrived(to_across[a, FAR], a, ACROSS_FAR)
        if a == 0:
            gate_up(PART, distant)
            transpose(2, hid, 2, 5)
            mixed_part(0)
    backward(PART, distant)
    gather = list(pending)

    def place(z, yr):
        d = ((zl + z) % 2) * 4 + (y + yr) % 4
        return pl.ds(pl.multiple_of(d * PANEL, PANEL), PANEL)

    def grad_term(z, source, rows):
        if source < 0:
            return mm(lt[rows, :], xc[0, :, place(z, 0)])
        cols = pl.ds(pl.multiple_of((zl + z) % 2 * PANEL, PANEL), PANEL)
        return mm(lty[source, rows, :], ry[source, :, cols])

    def quarter(lane, part):
        return pl.ds(lane * PANEL + part * QROWS, QROWS)

    def grad_down(z, yr):
        total = mm(lt[2 * PANEL:, :], xc[1, :, place(z, yr)]).astype(BF16)
        if z:
            pdo[yr] = total
        else:
            wd[:, yr * PANEL:(yr + 1) * PANEL] = total

    class Ring:
        def __init__(self, own, spare, right, left, rows, step):
            self.own, self.spare, self.right, self.left = own, spare, right, left
            self.rows, self.step = rows, step

        def far_lane(self, lane):
            copy = message(self.own(lane, 2), self.spare(0, lane), (self.right, self.left)[lane])
            setattr(self, ("far0", "far1")[lane], copy)
            copy.start()

        def far(self):
            self.far_lane(0)
            self.far_lane(1)

        def near(self):
            own, spare = self.own, self.spare
            self.near1 = message(own(1, 1), spare(1, 1), self.right)
            self.near0 = message(own(0, 3), spare(1, 0), self.left)
            self.near1.start()
            self.near0.start()

        def pass_on(self):
            own, spare = self.own, self.spare
            self.far0.wait_recv()
            add_into(own(0, 1), spare(0, 0), self.rows, self.step)
            self.last0 = message(own(0, 1), spare(2, 0), self.right)
            self.last0.start()
            self.far1.wait_recv()
            add_into(own(1, 3), spare(0, 1), self.rows, self.step)
            self.last1 = message(own(1, 3), spare(2, 1), self.left)
            self.last1.start()

        def finish(self, lane, extra=()):
            (self.near0, self.near1)[lane].wait_recv()
            (self.last0, self.last1)[lane].wait_recv()
            spare = self.spare
            mine = self.own(lane, 0)
            sum_to(mine, (mine, spare(1, lane), spare(2, lane)) + tuple(extra), self.rows, self.step)

    def down_ring(n, own):
        return Ring(own, lambda kind, lane: dring.at[n, kind, lane], y_right, y_left, QROWS // 2, 64)

    def lower(lane):
        return pl.ds(QROWS + lane * (QROWS // 2), QROWS // 2)

    down_a = down_ring(0, lambda lane, yr: wd.at[pl.ds(lane * (QROWS // 2), QROWS // 2), pl.ds(yr * PANEL, PANEL)])
    down_b = [
        down_ring(1, lambda lane, yr: wd.at[lower(lane), pl.ds(yr * PANEL, PANEL)]),
        down_ring(2, lambda lane, yr: pdo.at[yr, lower(lane), :]),
    ]

    slot_of = ((OWN, RIGHT, FAR, LEFT), (ACROSS, ACROSS_RIGHT, ACROSS_FAR, ACROSS_LEFT))

    def token_rows(m, slot, cols):
        rows = pl.ds(slot * BLOCK, BLOCK)
        return am.at[rows, cols] if m == 0 else xc.at[1, rows, cols]

    def token_ring(m, z):
        return Ring(
            lambda lane, xr: token_rows(m, slot_of[z][xr], pl.ds(lane * LANE, LANE)),
            lambda kind, lane: mring.at[m, z, kind, lane],
            x_right, x_left, BLOCK, 16,
        )

    tr = {(m, z): token_ring(m, z) for m in (0, 1) for z in (0, 1)}

    def half(ref, lane):
        return ref.at[pl.ds(lane * PANEL, PANEL), :]

    l_right = [message(half(lt, lane), half(lty.at[2], lane), y_right) for lane in (0, 1)]
    l_left = [message(half(lt, lane), half(lty.at[0], lane), y_left) for lane in (0, 1)]
    transpose(0, dg, 2, 5)
    l_right[0].start()
    transpose(1, du, 2, 5)
    l_left[1].start()
    l_right[1].start()
    l_left[0].start()
    down_z = {}
    for yr in (2, 1, 3, 0):
        grad_down(1, yr)
        down_z[yr] = message(pdo.at[yr, pl.ds(0, QROWS), :], dz.at[yr], z_next)
        down_z[yr].start()
    mixed_part(PART)
    mixed_over = [message(mb.at[j], sm.at[j], sibling) for j in range(4)]
    for copy in mixed_over:
        copy.start()
    for yr in (2, 1, 3, 0):
        grad_down(0, yr)
    for j in range(4):
        mixed_over[j].wait_recv()
        add_into(am.at[:, pl.ds(j * PANEL, PANEL)], sm.at[j], ROWS, 64)
    pl.semaphore_signal(credit, inc=1, device_id=sibling, device_id_type=MESH)
    tr[0, 1].far()
    tr[0, 1].near()
    for copy in gather:
        wait_send(copy)

    def input_grad(base, j):
        w = pl.ds(pl.multiple_of(base * HALF + j * PANEL, PANEL), PANEL)
        return (mm_nt(dg[...], wg[w, :]) + mm_nt(du[...], wu[w, :])).astype(BF16)

    @pl.loop(0, 4)
    def _(j):
        xc[1, :, pl.ds(pl.multiple_of(HALF + j * PANEL, PANEL), PANEL)] = input_grad(1 - c, j)

    pl.semaphore_wait(credit, 1)
    ig_over = [message(xc.at[1, :, pl.ds(HALF + j * PANEL, PANEL)], sm.at[j], sibling) for j in range(4)]
    for copy in ig_over:
        copy.start()

    @pl.loop(0, 4)
    def _(j):
        xc[1, :, pl.ds(pl.multiple_of(j * PANEL, PANEL), PANEL)] = input_grad(c, j)

    l_far = {}
    for lane, source, device in ((0, 2, y_right), (1, 0, y_left)):
        (l_right, l_left)[lane][lane].wait_recv()
        for part in (0, 1):
            rows = quarter(lane, part)
            l_far[lane, part] = message(lty.at[source, rows, :], lty.at[1, rows, :], device)
            l_far[lane, part].start()
    tr[0, 1].pass_on()
    for j in range(4):
        ig_over[j].wait_recv()
        add_into(xc.at[1, :, pl.ds(j * PANEL, PANEL)], sm.at[j], ROWS, 64)
    tr[1, 1].far()
    tr[1, 1].near()
    down_b[1].far()
    down_b[1].near()
    r_over = []
    for source in (0, 2, 1):
        for slot in range(8):
            r_sent[3 - source, slot].wait_recv()
        columns_held = ry.at[source, :, r_half]
        copy = message(columns_held, columns_held, sibling)
        copy.start()
        r_over.append(copy)

    def accumulate(source, rows):
        acc[rows, :] = grad_term(1, source, rows) if source < 0 else acc[rows, :] + grad_term(1, source, rows)

    for lane in (0, 1):
        accumulate(-1, pl.ds(lane * PANEL, PANEL))

    token_z = {}

    def send_across(m):
        for lane in (0, 1):
            tr[m, 1].finish(lane)
        token_z[m] = message(token_rows(m, ACROSS, pl.ds(0, HALF)), mz.at[m], z_across)
        token_z[m].start()

    def down_step(yr):
        down_z[yr].wait_recv()
        add_into(wd.at[pl.ds(0, QROWS), pl.ds(yr * PANEL, PANEL)], dz.at[yr], QROWS, 64)

    send_across(0)
    tr[1, 1].pass_on()
    for m in (0, 1):
        tr[m, 0].far()
        tr[m, 0].near()
    for copy in r_over:
        copy.wait_recv()
    l_left[0].wait_recv()
    l_right[1].wait_recv()
    for source in (0, 2):
        for lane in (0, 1):
            accumulate(source, pl.ds(lane * PANEL, PANEL))
    send_across(1)
    gate_z = {}
    for part in (0, 1):
        for lane in (0, 1):
            rows = quarter(lane, part)
            l_far[lane, part].wait_recv()
            gzs[rows, :] = (acc[rows, :] + grad_term(1, 1, rows)).astype(BF16)
            gate_z[lane, part] = message(gzs.at[rows, :], gz.at[rows, :], z_next)
            gate_z[lane, part].start()
    down_b[1].pass_on()
    for yr in (2, 1, 3, 0):
        down_step(yr)
    for ring in (down_a, down_b[0]):
        ring.far()
        ring.near()
    for m in (0, 1):
        tr[m, 0].pass_on()
    for lane in (0, 1):
        down_b[1].finish(lane)
    down_b_z = message(pdo.at[0, pl.ds(QROWS, QROWS), :], dbz, z_next)
    down_b_z.start()
    down_a.pass_on()
    down_b[0].pass_on()

    @pl.loop(0, 2)
    def _(lane):
        rows = pl.ds(pl.multiple_of(lane * PANEL, PANEL), PANEL)
        acc[rows, :] = grad_term(0, -1, rows) + grad_term(0, 0, rows) + grad_term(0, 1, rows) + grad_term(0, 2, rows)

    outs = []
    for m, out in enumerate((mixed_out, ig_out)):
        for lane in (0, 1):
            tr[m, 0].finish(lane)
        token_z[m].wait_recv()
        rows = token_rows(m, OWN, pl.ds(0, HALF))

        @pl.loop(0, 4)
        def _(j, m=m, rows=rows):
            cols = pl.ds(pl.multiple_of(j * PANEL, PANEL), PANEL)
            total = rows[:, cols].astype(F32) + mz[m, :, cols].astype(F32)
            top, bottom = total[:BLOCK // 2], total[BLOCK // 2:]
            fo[m, 0, :, cols] = jnp.where(c == 0, top, bottom).astype(BF16)
            fo[m, 1, :, cols] = jnp.where(c == 0, bottom, top).astype(BF16)

        keep = pltpu.make_async_copy(fo.at[m, 0], out.at[:, mine], local_sem.at[5 + m])
        give = message(fo.at[m, 1], out.at[:, mine], sibling)
        keep.start()
        give.start()
        outs.append((keep, give))

    grads = []
    for part in (0, 1):
        for lane in (0, 1):
            rows = quarter(lane, part)
            gate_z[lane, part].wait_recv()
            total = (acc[rows, :] + gz[rows, :].astype(F32)).astype(BF16)
            fin[lane, :, part * QROWS:(part + 1) * QROWS] = total.T
    for lane, out in enumerate((gate_out, up_out)):
        copy = pltpu.make_async_copy(fin.at[lane], out, local_sem.at[7 + lane])
        copy.start()
        grads.append(copy)
    for lane in (0, 1):
        down_a.finish(lane)
    down_b_z.wait_recv()
    for lane in (0, 1):
        down_b[0].finish(lane, (dbz.at[pl.ds(lane * (QROWS // 2), QROWS // 2), :],))
    copy = pltpu.make_async_copy(wd.at[:, pl.ds(0, PANEL)], down_out, local_sem.at[9])
    copy.start()
    grads.append(copy)

    for keep, give in outs:
        keep.wait()
        give.wait_recv()
    for copy in grads:
        copy.wait()
    for copy in pending:
        wait_send(copy)


def arrange(*refs):
    sources, results, held, sem = refs[:5], refs[5:10], refs[10:15], refs[15]
    ins = [pltpu.make_async_copy(sources[n], held[n], sem.at[n]) for n in range(5)]
    outs = [pltpu.make_async_copy(held[n], results[n], sem.at[5 + n]) for n in range(5)]
    for copy in ins:
        copy.start()
    for n in range(5):
        ins[n].wait()
        outs[n].start()
    for copy in outs:
        copy.wait()


def on_device(tokens, w_gate, w_up, w_down, cotangent):
    v = lambda *shape: pltpu.VMEM(shape, BF16)
    shapes = [jax.ShapeDtypeStruct((BLOCK // 2, D), BF16)] * 2 + [jax.ShapeDtypeStruct((PANEL, PANEL), BF16)] * 3
    results = pl.pallas_call(
        kernel,
        out_shape=shapes,
        in_specs=[pl.BlockSpec(memory_space=pl.ANY)] * 5,
        out_specs=[pl.BlockSpec(memory_space=pl.ANY)] * 5,
        scratch_shapes=[
            v(D, PANEL), v(D, PANEL), v(PANEL, D),
            v(2, ROWS, D),
            v(ROWS, PANEL), v(ROWS, PANEL), v(ROWS, PANEL),
            v(3 * PANEL, ROWS),
            pltpu.VMEM((PART, PANEL), F32), pltpu.VMEM((PART, PANEL), F32), pltpu.VMEM((PART, PANEL), F32),
            v(ROWS, HALF), v(4, ROWS, PANEL), v(4, ROWS, PANEL), v(4, PANEL, PANEL),
            v(2, 2, 3, 2, BLOCK, LANE), v(2, BLOCK, HALF),
            v(3, ROWS, 2 * PANEL), v(3, 2 * PANEL, ROWS),
            pltpu.VMEM((2 * PANEL, PANEL), F32), v(2 * PANEL, PANEL), v(2 * PANEL, PANEL), v(2, PANEL, PANEL),
            v(4, QROWS, PANEL), v(QROWS, PANEL), v(3, 3, 2, QROWS // 2, PANEL),
            v(2, 2, BLOCK // 2, HALF), v(2, 2, BLOCK // 2, HALF),
            pltpu.SemaphoreType.DMA((MESSAGES,)),
            pltpu.SemaphoreType.DMA((MESSAGES,)),
            pltpu.SemaphoreType.DMA((10,)),
            pltpu.SemaphoreType.REGULAR,
        ],
        compiler_params=pltpu.CompilerParams(
            collective_id=0, has_side_effects=True, vmem_limit_bytes=63 * 1024 * 1024
        ),
        cost_estimate=pl.CostEstimate(flops=24_200_000_000, bytes_accessed=16_000_000, transcendentals=330_000),
    )(tokens, w_gate, w_up, w_down, cotangent)
    return pl.pallas_call(
        arrange,
        out_shape=shapes,
        in_specs=[pl.BlockSpec(memory_space=pl.ANY)] * 5,
        out_specs=[pl.BlockSpec(memory_space=pl.ANY)] * 5,
        scratch_shapes=[pltpu.VMEM(shape.shape, BF16) for shape in shapes] + [pltpu.SemaphoreType.DMA((10,))],
        compiler_params=pltpu.CompilerParams(vmem_limit_bytes=60 * 1024 * 1024),
    )(*results)


def solution(mesh):
    in_specs = (
        P(("dp", "mp"), None),
        P(None, "mp"),
        P(None, "mp"),
        P("mp", None),
        P(("dp", "mp"), None),
    )
    out_specs = (
        P(("dp", "mp"), None),
        P(("dp", "mp"), None),
        P("dp", "mp"),
        P("dp", "mp"),
        P("mp", "dp"),
    )
    return jax.shard_map(
        on_device, mesh=mesh, in_specs=in_specs, out_specs=out_specs, check_vma=False
    )
```

```python
import jax
import jax.numpy as jnp
from jax import lax
from jax.experimental import pallas as pl
from jax.experimental.pallas import tpu as pltpu
from jax.sharding import PartitionSpec as P

MESH = pl.DeviceIdType.MESH
BF16 = jnp.bfloat16
F32 = jnp.float32
D = 4096
HALF = D // 2
LANE = HALF // 2
PANEL = 512
ROWS = 640
BLOCK = 80
FIRST = 240
MOST = 400
MESSAGES = 160
QROWS = PANEL // 2

OWN, LEFT, ACROSS, RIGHT, FAR, ACROSS_LEFT, ACROSS_RIGHT, ACROSS_FAR = range(8)


def mm(a, b):
    return jnp.dot(a, b, preferred_element_type=F32)


def mm_nt(a, b):
    return lax.dot_general(a, b, (((1,), (1,)), ((), ())), preferred_element_type=F32)


def add_into(dst, src, rows, step):
    @pl.loop(0, rows // step)
    def _(i):
        r = pl.ds(pl.multiple_of(i * step, step), step)
        dst[r, :] = (dst[r, :].astype(F32) + src[r, :].astype(F32)).astype(BF16)


def sum_to(dst, terms, rows, step):
    @pl.loop(0, rows // step)
    def _(i):
        r = pl.ds(pl.multiple_of(i * step, step), step)
        total = terms[0][r, :].astype(F32)
        for term in terms[1:]:
            total += term[r, :].astype(F32)
        dst[r, :] = total.astype(BF16)


def kernel(
    tok_hbm, wg_hbm, wu_hbm, wd_hbm, cot_hbm,
    mixed_out, ig_out, gate_out, up_out, down_out,
    wg, wu, wd, xc, hid, dg, du, lt, gf, uf, df, am, mb, sm, pdo,
    mring, mz, ry, lty, acc, gzs, gz, fin, dz, dbz, dring, t_in, t_next, fo,
    send_sem, recv_sem, local_sem, credit,
):
    dp, mp = lax.axis_index("dp"), lax.axis_index("mp")
    zl, y = dp // 4, dp % 4
    zh, x, c = mp // 8, (mp // 2) % 4, mp % 2
    x_right = (dp, zh * 8 + ((x + 1) % 4) * 2 + c)
    x_left = (dp, zh * 8 + ((x + 3) % 4) * 2 + c)
    z_across = (dp, (1 - zh) * 8 + x * 2 + c)
    sibling = (dp, zh * 8 + x * 2 + (1 - c))
    y_right = (zl * 4 + (y + 1) % 4, mp)
    y_left = (zl * 4 + (y + 3) % 4, mp)
    y_far = (zl * 4 + (y + 2) % 4, mp)
    z_next = ((1 - zl) * 4 + y, mp)
    mine = pl.ds(pl.multiple_of(c * HALF, HALF), HALF)
    other = pl.ds(pl.multiple_of((1 - c) * HALF, HALF), HALF)

    pending = []

    def message(src, dst, device):
        n = len(pending)
        copy = pltpu.make_async_remote_copy(
            src_ref=src, dst_ref=dst, send_sem=send_sem.at[n], recv_sem=recv_sem.at[n],
            device_id=device, device_id_type=MESH,
        )
        pending.append(copy)
        return copy

    sent = set()

    def wait_send(copy):
        if id(copy) not in sent:
            sent.add(id(copy))
            copy.wait_send()

    weights = [
        pltpu.make_async_copy(src, dst, local_sem.at[n])
        for n, (src, dst) in enumerate(((wg_hbm, wg), (wu_hbm, wu), (wd_hbm, wd)))
    ]
    inputs = (tok_hbm, cot_hbm)
    own_rows = [pltpu.make_async_copy(inputs[a].at[:, mine], t_in.at[c, a], local_sem.at[3 + a]) for a in (0, 1)]
    for copy in own_rows:
        copy.start()

    barrier = pltpu.get_barrier_semaphore()
    partners = (x_right, x_left, z_across, sibling, y_right, y_left, y_far, z_next)
    for device in partners:
        pl.semaphore_signal(barrier, inc=1, device_id=device, device_id_type=MESH)
    pl.semaphore_wait(barrier, len(partners))

    rows_over = [message(inputs[a].at[:, other], t_in.at[c, a], sibling) for a in (0, 1)]
    for copy in rows_over:
        copy.start()

    def block(a, slot, cols=mine):
        return xc.at[a, pl.ds(slot * BLOCK, BLOCK), cols]

    r_half = pl.ds(pl.multiple_of(c * PANEL, PANEL), PANEL)
    r_sent = {}

    def send_columns(slot):
        rows = pl.ds(slot * BLOCK, BLOCK)
        for yr, device in ((1, y_right), (3, y_left), (2, y_far)):
            cols = pl.ds(pl.multiple_of(c * HALF + (y + yr) % 4 * PANEL, PANEL), PANEL)
            r_sent[yr, slot] = message(xc.at[0, rows, cols], ry.at[3 - yr, rows, r_half], device)
            r_sent[yr, slot].start()

    def hand_over(a, slot):
        copy = message(block(a, slot), block(a, slot), sibling)
        copy.start()
        if a == 0:
            send_columns(slot)
        return copy

    parts = [pl.ds(pl.multiple_of(c * HALF + i * LANE, LANE), LANE) for i in (0, 1)]
    to_right, to_left, to_across, relay, over = {}, {}, {}, {}, {}

    def first_out(a, core):
        copy = message(t_in.at[core, a], t_next.at[a, core], (x_right, x_left)[a])
        copy.start()
        return copy

    def join(halves, a, slot):
        @pl.loop(0, HALF // PANEL)
        def _(j):
            cols = pl.ds(pl.multiple_of(j * PANEL, PANEL), PANEL)
            both = jnp.concatenate([halves(0)[:, cols].astype(F32), halves(1)[:, cols].astype(F32)], axis=0)
            to = pl.ds(pl.multiple_of(c * HALF + j * PANEL, PANEL), PANEL)
            xc[a, slot * BLOCK:(slot + 1) * BLOCK, to] = both.astype(BF16)

    early = []
    for a in (0, 1):
        own_rows[a].wait()
        early.append([first_out(a, c)])
    for a in (0, 1):
        rows_over[a].wait_recv()
        early[a].append(first_out(a, 1 - c))
        join(lambda core, a=a: t_in.at[core, a], a, OWN)
        to_across[a, OWN] = message(block(a, OWN), block(a, ACROSS), z_across)
        if a == 1:
            to_right[1, OWN] = [message(block(1, OWN, cols), block(1, LEFT, cols), x_right) for cols in parts]
            to_left[0, OWN] = [message(block(0, OWN, cols), block(0, RIGHT, cols), x_left) for cols in parts]
            to_right[1, OWN][0].start()
            to_left[0, OWN][0].start()
        to_across[a, OWN].start()
        over[a, OWN] = hand_over(a, OWN)
    for copy in weights:
        copy.start()

    def relay_far(a):
        if a == 0:
            relay[a] = message(block(a, LEFT), block(a, FAR), x_right)
        else:
            relay[a] = message(block(a, RIGHT), block(a, FAR), x_left)
        relay[a].start()

    def from_across(a):
        to_across[a, OWN].wait_recv()
        to_right[a, ACROSS] = message(block(a, ACROSS), block(a, ACROSS_LEFT), x_right)
        to_left[a, ACROSS] = message(block(a, ACROSS), block(a, ACROSS_RIGHT), x_left)
        to_right[a, ACROSS].start()
        to_left[a, ACROSS].start()
        over[a, ACROSS] = hand_over(a, ACROSS)

    def from_far(a):
        relay[a].wait_recv()
        to_across[a, FAR] = message(block(a, FAR), block(a, ACROSS_FAR), z_across)
        to_across[a, FAR].start()
        over[a, FAR] = hand_over(a, FAR)

    def arrived(copy, a, slot):
        copy.wait_recv()
        over[a, slot] = hand_over(a, slot)

    def wait_over(a, slots):
        for slot in slots:
            over[a, slot].wait_recv()

    def columns(k):
        return pl.ds(pl.multiple_of((c * 2 + k) % 4 * 1024, 1024), 1024)

    def gate_up(r0, count, slots):
        span = pl.ds(r0, count)
        gf[span, :] = jnp.zeros((count, PANEL), F32)
        uf[span, :] = jnp.zeros((count, PANEL), F32)

        def step(k):
            ks = columns(k)
            rows = xc[0, span, ks]
            gf[span, :] += mm(rows, wg[ks, :])
            uf[span, :] += mm(rows, wu[ks, :])

        pl.loop(0, 2)(step)
        wait_over(0, slots)
        pl.loop(2, 4)(step)

        @pl.loop(0, count // 16)
        def _(i):
            r = pl.ds(pl.multiple_of(r0 + i * 16, 16), 16)
            gate, up = gf[r, :], uf[r, :]
            s = 1.0 / (1.0 + jnp.exp(-gate))
            swish = gate * s
            hid[r, :] = (swish * up).astype(BF16)
            gf[r, :] = up * s * (1.0 + gate * (1.0 - s))
            uf[r, :] = swish

    def backward(r0, count, slots):
        span = pl.ds(0, count)
        df[span, :] = jnp.zeros((count, PANEL), F32)

        def step(k):
            ks = columns(k)
            df[span, :] += mm_nt(xc[1, r0:r0 + count, ks], wd[:, ks])

        pl.loop(0, 2)(step)
        wait_over(1, slots)
        pl.loop(2, 4)(step)

        @pl.loop(0, count // 16)
        def _(i):
            r = pl.ds(pl.multiple_of(r0 + i * 16, 16), 16)
            dhidden = df[pl.ds(pl.multiple_of(i * 16, 16), 16), :]
            dg[r, :] = (dhidden * gf[r, :]).astype(BF16)
            du[r, :] = (dhidden * uf[r, :]).astype(BF16)

    def mixed_sums():
        @pl.loop(0, 4)
        def _(j):
            cols = pl.ds(pl.multiple_of((1 - c) * HALF + j * PANEL, PANEL), PANEL)
            mb[j] = mm(hid[...], wd[:, cols]).astype(BF16)

        @pl.loop(0, 4)
        def _(j):
            cols = pl.ds(pl.multiple_of(c * HALF + j * PANEL, PANEL), PANEL)
            total = mm(hid[...], wd[:, cols]).astype(BF16)
            am[:, pl.ds(pl.multiple_of(j * PANEL, PANEL), PANEL)] = total

    def transpose(q, src, start, stop):
        for i in range(start, stop):
            lt[q * PANEL:(q + 1) * PANEL, i * 128:(i + 1) * 128] = src[i * 128:(i + 1) * 128, :].T

    def first_in(a, slot):
        for copy in early[a]:
            copy.wait_recv()
        join(lambda core: t_next.at[a, core], a, slot)

    first_in(0, LEFT)
    relay_far(0)
    to_right[1, OWN][1].start()
    first_in(1, RIGHT)
    relay_far(1)
    to_left[0, OWN][1].start()
    over[0, LEFT] = hand_over(0, LEFT)
    over[1, RIGHT] = hand_over(1, RIGHT)
    from_across(0)
    from_across(1)
    weights[0].wait()
    weights[1].wait()
    gate_up(0, FIRST, (OWN, LEFT, ACROSS))
    from_far(0)
    from_far(1)
    for a, slot, halves in ((0, RIGHT, to_left[0, OWN]), (1, LEFT, to_right[1, OWN])):
        halves[0].wait_recv()
        arrived(halves[1], a, slot)
    gate_up(FIRST, MOST - FIRST, (RIGHT, FAR))
    weights[2].wait()
    backward(0, MOST, (OWN, LEFT, ACROSS, RIGHT, FAR))
    for q, src in enumerate((dg, du, hid)):
        transpose(q, src, 0, 3)
    distant = (ACROSS_LEFT, ACROSS_RIGHT, ACROSS_FAR)
    for a in (0, 1):
        arrived(to_left[a, ACROSS], a, ACROSS_RIGHT)
        arrived(to_right[a, ACROSS], a, ACROSS_LEFT)
        arrived(to_across[a, FAR], a, ACROSS_FAR)
        if a == 0:
            gate_up(MOST, ROWS - MOST, distant)
    backward(MOST, ROWS - MOST, distant)
    gather = list(pending)

    def place(z, yr):
        d = ((zl + z) % 2) * 4 + (y + yr) % 4
        return pl.ds(pl.multiple_of(d * PANEL, PANEL), PANEL)

    def grad_term(z, source, rows):
        if source < 0:
            return mm(lt[rows, :], xc[0, :, place(z, 0)])
        cols = pl.ds(pl.multiple_of((zl + z) % 2 * PANEL, PANEL), PANEL)
        return mm(lty[source, rows, :], ry[source, :, cols])

    def quarter(lane, part):
        return pl.ds(lane * PANEL + part * QROWS, QROWS)

    def grad_down(z, yr):
        total = mm(lt[2 * PANEL:, :], xc[1, :, place(z, yr)]).astype(BF16)
        if z:
            pdo[yr] = total
        else:
            wd[:, yr * PANEL:(yr + 1) * PANEL] = total

    class Ring:
        def __init__(self, own, spare, right, left, rows, step):
            self.own, self.spare, self.right, self.left = own, spare, right, left
            self.rows, self.step = rows, step

        def far_lane(self, lane):
            copy = message(self.own(lane, 2), self.spare(0, lane), (self.right, self.left)[lane])
            setattr(self, ("far0", "far1")[lane], copy)
            copy.start()

        def far(self):
            self.far_lane(0)
            self.far_lane(1)

        def near(self):
            own, spare = self.own, self.spare
            self.near1 = message(own(1, 1), spare(1, 1), self.right)
            self.near0 = message(own(0, 3), spare(1, 0), self.left)
            self.near1.start()
            self.near0.start()

        def pass_on(self):
            own, spare = self.own, self.spare
            self.far0.wait_recv()
            add_into(own(0, 1), spare(0, 0), self.rows, self.step)
            self.last0 = message(own(0, 1), spare(2, 0), self.right)
            self.last0.start()
            self.far1.wait_recv()
            add_into(own(1, 3), spare(0, 1), self.rows, self.step)
            self.last1 = message(own(1, 3), spare(2, 1), self.left)
            self.last1.start()

        def finish(self, lane, extra=()):
            (self.near0, self.near1)[lane].wait_recv()
            (self.last0, self.last1)[lane].wait_recv()
            spare = self.spare
            mine = self.own(lane, 0)
            sum_to(mine, (mine, spare(1, lane), spare(2, lane)) + tuple(extra), self.rows, self.step)

    def down_ring(n, own):
        return Ring(own, lambda kind, lane: dring.at[n, kind, lane], y_right, y_left, QROWS // 2, 64)

    def lower(lane):
        return pl.ds(QROWS + lane * (QROWS // 2), QROWS // 2)

    down_a = down_ring(0, lambda lane, yr: wd.at[pl.ds(lane * (QROWS // 2), QROWS // 2), pl.ds(yr * PANEL, PANEL)])
    down_b = [
        down_ring(1, lambda lane, yr: wd.at[lower(lane), pl.ds(yr * PANEL, PANEL)]),
        down_ring(2, lambda lane, yr: pdo.at[yr, lower(lane), :]),
    ]

    slot_of = ((OWN, RIGHT, FAR, LEFT), (ACROSS, ACROSS_RIGHT, ACROSS_FAR, ACROSS_LEFT))

    def token_rows(m, slot, cols):
        rows = pl.ds(slot * BLOCK, BLOCK)
        return am.at[rows, cols] if m == 0 else xc.at[1, rows, cols]

    def token_ring(m, z):
        return Ring(
            lambda lane, xr: token_rows(m, slot_of[z][xr], pl.ds(lane * LANE, LANE)),
            lambda kind, lane: mring.at[m, z, kind, lane],
            x_right, x_left, BLOCK, 16,
        )

    tr = {(m, z): token_ring(m, z) for m in (0, 1) for z in (0, 1)}

    def half(ref, lane):
        return ref.at[pl.ds(lane * PANEL, PANEL), :]

    l_right = [message(half(lt, lane), half(lty.at[2], lane), y_right) for lane in (0, 1)]
    l_left = [message(half(lt, lane), half(lty.at[0], lane), y_left) for lane in (0, 1)]
    transpose(0, dg, 3, 5)
    l_right[0].start()
    transpose(1, du, 3, 5)
    l_left[1].start()
    l_right[1].start()
    l_left[0].start()
    transpose(2, hid, 3, 5)
    down_z = {}
    for yr in (2, 1, 3, 0):
        grad_down(1, yr)
        down_z[yr] = message(pdo.at[yr, pl.ds(0, QROWS), :], dz.at[yr], z_next)
        down_z[yr].start()
    mixed_sums()
    mixed_over = [message(mb.at[j], sm.at[j], sibling) for j in range(4)]
    for copy in mixed_over:
        copy.start()
    for yr in (2, 1, 3, 0):
        grad_down(0, yr)
    for j in range(4):
        mixed_over[j].wait_recv()
        add_into(am.at[:, pl.ds(j * PANEL, PANEL)], sm.at[j], ROWS, 64)
    pl.semaphore_signal(credit, inc=1, device_id=sibling, device_id_type=MESH)
    tr[0, 1].far()
    tr[0, 1].near()
    for copy in gather:
        wait_send(copy)

    def input_grad(base, j):
        w = pl.ds(pl.multiple_of(base * HALF + j * PANEL, PANEL), PANEL)
        return (mm_nt(dg[...], wg[w, :]) + mm_nt(du[...], wu[w, :])).astype(BF16)

    @pl.loop(0, 4)
    def _(j):
        xc[1, :, pl.ds(pl.multiple_of(HALF + j * PANEL, PANEL), PANEL)] = input_grad(1 - c, j)

    pl.semaphore_wait(credit, 1)
    ig_over = [message(xc.at[1, :, pl.ds(HALF + j * PANEL, PANEL)], sm.at[j], sibling) for j in range(4)]
    for copy in ig_over:
        copy.start()
    tr[0, 1].pass_on()

    @pl.loop(0, 4)
    def _(j):
        xc[1, :, pl.ds(pl.multiple_of(j * PANEL, PANEL), PANEL)] = input_grad(c, j)

    token_z = {}

    def send_across(m):
        for lane in (0, 1):
            tr[m, 1].finish(lane)
        token_z[m] = message(token_rows(m, ACROSS, pl.ds(0, HALF)), mz.at[m], z_across)
        token_z[m].start()

    l_far = {}
    for lane, source, device in ((0, 2, y_right), (1, 0, y_left)):
        (l_right, l_left)[lane][lane].wait_recv()
        for part in (0, 1):
            rows = quarter(lane, part)
            l_far[lane, part] = message(lty.at[source, rows, :], lty.at[1, rows, :], device)
            l_far[lane, part].start()
    for j in range(4):
        ig_over[j].wait_recv()
        add_into(xc.at[1, :, pl.ds(j * PANEL, PANEL)], sm.at[j], ROWS, 64)
    tr[1, 1].far()
    tr[1, 1].near()
    down_b[1].far()
    down_b[1].near()
    send_across(0)
    r_over = []
    for source in (0, 2, 1):
        for slot in range(8):
            r_sent[3 - source, slot].wait_recv()
        columns_held = ry.at[source, :, r_half]
        copy = message(columns_held, columns_held, sibling)
        copy.start()
        r_over.append(copy)

    def accumulate(source, rows):
        acc[rows, :] = grad_term(1, source, rows) if source < 0 else acc[rows, :] + grad_term(1, source, rows)

    for lane in (0, 1):
        accumulate(-1, pl.ds(lane * PANEL, PANEL))

    def down_step(yr):
        down_z[yr].wait_recv()
        add_into(wd.at[pl.ds(0, QROWS), pl.ds(yr * PANEL, PANEL)], dz.at[yr], QROWS, 64)

    tr[1, 1].pass_on()
    for m in (0, 1):
        tr[m, 0].far()
        tr[m, 0].near()
    for copy in r_over:
        copy.wait_recv()
    l_left[0].wait_recv()
    l_right[1].wait_recv()
    for source in (0, 2):
        for lane in (0, 1):
            accumulate(source, pl.ds(lane * PANEL, PANEL))
    send_across(1)
    gate_z = {}
    for part in (0, 1):
        for lane in (0, 1):
            rows = quarter(lane, part)
            l_far[lane, part].wait_recv()
            gzs[rows, :] = (acc[rows, :] + grad_term(1, 1, rows)).astype(BF16)
            gate_z[lane, part] = message(gzs.at[rows, :], gz.at[rows, :], z_next)
            gate_z[lane, part].start()
    down_b[1].pass_on()
    for yr in (2, 1, 3, 0):
        down_step(yr)
    for ring in (down_a, down_b[0]):
        ring.far()
        ring.near()
    for m in (0, 1):
        tr[m, 0].pass_on()

    @pl.loop(0, 2)
    def _(lane):
        rows = pl.ds(pl.multiple_of(lane * PANEL, PANEL), PANEL)
        acc[rows, :] = grad_term(0, -1, rows) + grad_term(0, 0, rows) + grad_term(0, 1, rows) + grad_term(0, 2, rows)

    for lane in (0, 1):
        down_b[1].finish(lane)
    down_b_z = message(pdo.at[0, pl.ds(QROWS, QROWS), :], dbz, z_next)
    down_b_z.start()
    down_a.pass_on()
    down_b[0].pass_on()

    outs = []
    for m, out in enumerate((mixed_out, ig_out)):
        for lane in (0, 1):
            tr[m, 0].finish(lane)
        token_z[m].wait_recv()
        rows = token_rows(m, OWN, pl.ds(0, HALF))

        @pl.loop(0, 4)
        def _(j, m=m, rows=rows):
            cols = pl.ds(pl.multiple_of(j * PANEL, PANEL), PANEL)
            total = rows[:, cols].astype(F32) + mz[m, :, cols].astype(F32)
            top, bottom = total[:BLOCK // 2], total[BLOCK // 2:]
            fo[m, 0, :, cols] = jnp.where(c == 0, top, bottom).astype(BF16)
            fo[m, 1, :, cols] = jnp.where(c == 0, bottom, top).astype(BF16)

        keep = pltpu.make_async_copy(fo.at[m, 0], out.at[:, mine], local_sem.at[5 + m])
        give = message(fo.at[m, 1], out.at[:, mine], sibling)
        keep.start()
        give.start()
        outs.append((keep, give))

    grads = []
    for part in (0, 1):
        for lane in (0, 1):
            rows = quarter(lane, part)
            gate_z[lane, part].wait_recv()
            total = (acc[rows, :] + gz[rows, :].astype(F32)).astype(BF16)
            fin[lane, :, part * QROWS:(part + 1) * QROWS] = total.T
    for lane, out in enumerate((gate_out, up_out)):
        copy = pltpu.make_async_copy(fin.at[lane], out, local_sem.at[7 + lane])
        copy.start()
        grads.append(copy)
    for lane in (0, 1):
        down_a.finish(lane)
    down_b_z.wait_recv()
    for lane in (0, 1):
        down_b[0].finish(lane, (dbz.at[pl.ds(lane * (QROWS // 2), QROWS // 2), :],))
    copy = pltpu.make_async_copy(wd.at[:, pl.ds(0, PANEL)], down_out, local_sem.at[9])
    copy.start()
    grads.append(copy)

    for keep, give in outs:
        keep.wait()
        give.wait_recv()
    for copy in grads:
        copy.wait()
    for copy in pending:
        wait_send(copy)


def arrange(*refs):
    sources, results, held, sem = refs[:5], refs[5:10], refs[10:15], refs[15]
    ins = [pltpu.make_async_copy(sources[n], held[n], sem.at[n]) for n in range(5)]
    outs = [pltpu.make_async_copy(held[n], results[n], sem.at[5 + n]) for n in range(5)]
    for copy in ins:
        copy.start()
    for n in range(5):
        ins[n].wait()
        outs[n].start()
    for copy in outs:
        copy.wait()


def on_device(tokens, w_gate, w_up, w_down, cotangent):
    v = lambda *shape: pltpu.VMEM(shape, BF16)
    shapes = [jax.ShapeDtypeStruct((BLOCK // 2, D), BF16)] * 2 + [jax.ShapeDtypeStruct((PANEL, PANEL), BF16)] * 3
    results = pl.pallas_call(
        kernel,
        out_shape=shapes,
        in_specs=[pl.BlockSpec(memory_space=pl.ANY)] * 5,
        out_specs=[pl.BlockSpec(memory_space=pl.ANY)] * 5,
        scratch_shapes=[
            v(D, PANEL), v(D, PANEL), v(PANEL, D),
            v(2, ROWS, D),
            v(ROWS, PANEL), v(ROWS, PANEL), v(ROWS, PANEL),
            v(3 * PANEL, ROWS),
            pltpu.VMEM((ROWS, PANEL), F32), pltpu.VMEM((ROWS, PANEL), F32), pltpu.VMEM((MOST, PANEL), F32),
            v(ROWS, HALF), v(4, ROWS, PANEL), v(4, ROWS, PANEL), v(4, PANEL, PANEL),
            v(2, 2, 3, 2, BLOCK, LANE), v(2, BLOCK, HALF),
            v(3, ROWS, 2 * PANEL), v(3, 2 * PANEL, ROWS),
            pltpu.VMEM((2 * PANEL, PANEL), F32), v(2 * PANEL, PANEL), v(2 * PANEL, PANEL), v(2, PANEL, PANEL),
            v(4, QROWS, PANEL), v(QROWS, PANEL), v(3, 3, 2, QROWS // 2, PANEL),
            v(2, 2, BLOCK // 2, HALF), v(2, 2, BLOCK // 2, HALF), v(2, 2, BLOCK // 2, HALF),
            pltpu.SemaphoreType.DMA((MESSAGES,)),
            pltpu.SemaphoreType.DMA((MESSAGES,)),
            pltpu.SemaphoreType.DMA((10,)),
            pltpu.SemaphoreType.REGULAR,
        ],
        compiler_params=pltpu.CompilerParams(
            collective_id=0, has_side_effects=True, vmem_limit_bytes=63 * 1024 * 1024
        ),
        cost_estimate=pl.CostEstimate(flops=24_200_000_000, bytes_accessed=16_000_000, transcendentals=330_000),
    )(tokens, w_gate, w_up, w_down, cotangent)
    return pl.pallas_call(
        arrange,
        out_shape=shapes,
        in_specs=[pl.BlockSpec(memory_space=pl.ANY)] * 5,
        out_specs=[pl.BlockSpec(memory_space=pl.ANY)] * 5,
        scratch_shapes=[pltpu.VMEM(shape.shape, BF16) for shape in shapes] + [pltpu.SemaphoreType.DMA((10,))],
        compiler_params=pltpu.CompilerParams(vmem_limit_bytes=60 * 1024 * 1024),
    )(*results)


def solution(mesh):
    in_specs = (
        P(("dp", "mp"), None),
        P(None, "mp"),
        P(None, "mp"),
        P("mp", None),
        P(("dp", "mp"), None),
    )
    out_specs = (
        P(("dp", "mp"), None),
        P(("dp", "mp"), None),
        P("dp", "mp"),
        P("dp", "mp"),
        P("mp", "dp"),
    )
    return jax.shard_map(
        on_device, mesh=mesh, in_specs=in_specs, out_specs=out_specs, check_vma=False
    )
```

```python
import jax
import jax.numpy as jnp
from jax import lax
from jax.experimental import pallas as pl
from jax.experimental.pallas import tpu as pltpu
from jax.sharding import PartitionSpec as P

MESH = pl.DeviceIdType.MESH
BF16 = jnp.bfloat16
F32 = jnp.float32
D = 4096
HALF = D // 2
LANE = HALF // 2
PANEL = 512
ROWS = 640
BLOCK = 80
FIRST = 240
MOST = 400
MESSAGES = 160
QROWS = PANEL // 2

OWN, LEFT, ACROSS, RIGHT, FAR, ACROSS_LEFT, ACROSS_RIGHT, ACROSS_FAR = range(8)


def mm(a, b):
    return jnp.dot(a, b, preferred_element_type=F32)


def mm_nt(a, b):
    return lax.dot_general(a, b, (((1,), (1,)), ((), ())), preferred_element_type=F32)


def add_into(dst, src, rows, step):
    @pl.loop(0, rows // step)
    def _(i):
        r = pl.ds(pl.multiple_of(i * step, step), step)
        dst[r, :] = (dst[r, :].astype(F32) + src[r, :].astype(F32)).astype(BF16)


def sum_to(dst, terms, rows, step):
    @pl.loop(0, rows // step)
    def _(i):
        r = pl.ds(pl.multiple_of(i * step, step), step)
        total = terms[0][r, :].astype(F32)
        for term in terms[1:]:
            total += term[r, :].astype(F32)
        dst[r, :] = total.astype(BF16)


def kernel(
    tok_hbm, wg_hbm, wu_hbm, wd_hbm, cot_hbm,
    mixed_out, ig_out, gate_out, up_out, down_out,
    wg, wu, wd, xc, hid, dg, du, lt, gf, uf, df, am, mb, sm, pdo,
    mring, mz, ry, lty, acc, gzs, gz, fin, dz, dbz, dring, t_in, t_next, fo,
    send_sem, recv_sem, local_sem, credit,
):
    dp, mp = lax.axis_index("dp"), lax.axis_index("mp")
    zl, y = dp // 4, dp % 4
    zh, x, c = mp // 8, (mp // 2) % 4, mp % 2
    x_right = (dp, zh * 8 + ((x + 1) % 4) * 2 + c)
    x_left = (dp, zh * 8 + ((x + 3) % 4) * 2 + c)
    z_across = (dp, (1 - zh) * 8 + x * 2 + c)
    sibling = (dp, zh * 8 + x * 2 + (1 - c))
    y_right = (zl * 4 + (y + 1) % 4, mp)
    y_left = (zl * 4 + (y + 3) % 4, mp)
    y_far = (zl * 4 + (y + 2) % 4, mp)
    z_next = ((1 - zl) * 4 + y, mp)
    mine = pl.ds(pl.multiple_of(c * HALF, HALF), HALF)
    other = pl.ds(pl.multiple_of((1 - c) * HALF, HALF), HALF)

    pending = []

    def message(src, dst, device):
        n = len(pending)
        copy = pltpu.make_async_remote_copy(
            src_ref=src, dst_ref=dst, send_sem=send_sem.at[n], recv_sem=recv_sem.at[n],
            device_id=device, device_id_type=MESH,
        )
        pending.append(copy)
        return copy

    sent = set()

    def wait_send(copy):
        if id(copy) not in sent:
            sent.add(id(copy))
            copy.wait_send()

    weights = [
        pltpu.make_async_copy(src, dst, local_sem.at[n])
        for n, (src, dst) in enumerate(((wg_hbm, wg), (wu_hbm, wu), (wd_hbm, wd)))
    ]
    inputs = (tok_hbm, cot_hbm)
    own_rows = [pltpu.make_async_copy(inputs[a].at[:, mine], t_in.at[c, a], local_sem.at[3 + a]) for a in (0, 1)]
    for copy in own_rows:
        copy.start()

    barrier = pltpu.get_barrier_semaphore()
    partners = (x_right, x_left, z_across, sibling, y_right, y_left, y_far, z_next)
    for device in partners:
        pl.semaphore_signal(barrier, inc=1, device_id=device, device_id_type=MESH)
    pl.semaphore_wait(barrier, len(partners))

    rows_over = [message(inputs[a].at[:, other], t_in.at[c, a], sibling) for a in (0, 1)]
    for copy in rows_over:
        copy.start()

    def block(a, slot, cols=mine):
        return xc.at[a, pl.ds(slot * BLOCK, BLOCK), cols]

    r_half = pl.ds(pl.multiple_of(c * PANEL, PANEL), PANEL)
    r_sent = {}

    def send_columns(slot):
        rows = pl.ds(slot * BLOCK, BLOCK)
        for yr, device in ((1, y_right), (3, y_left), (2, y_far)):
            cols = pl.ds(pl.multiple_of(c * HALF + (y + yr) % 4 * PANEL, PANEL), PANEL)
            r_sent[yr, slot] = message(xc.at[0, rows, cols], ry.at[3 - yr, rows, r_half], device)
            r_sent[yr, slot].start()

    def hand_over(a, slot):
        copy = message(block(a, slot), block(a, slot), sibling)
        copy.start()
        if a == 0:
            send_columns(slot)
        return copy

    parts = [pl.ds(pl.multiple_of(c * HALF + i * LANE, LANE), LANE) for i in (0, 1)]
    to_right, to_left, to_across, relay, over = {}, {}, {}, {}, {}

    def first_out(a, core):
        copy = message(t_in.at[core, a], t_next.at[a, core], (x_right, x_left)[a])
        copy.start()
        return copy

    def join(halves, a, slot):
        @pl.loop(0, HALF // PANEL)
        def _(j):
            cols = pl.ds(pl.multiple_of(j * PANEL, PANEL), PANEL)
            both = jnp.concatenate([halves(0)[:, cols].astype(F32), halves(1)[:, cols].astype(F32)], axis=0)
            to = pl.ds(pl.multiple_of(c * HALF + j * PANEL, PANEL), PANEL)
            xc[a, slot * BLOCK:(slot + 1) * BLOCK, to] = both.astype(BF16)

    early = []
    for a in (0, 1):
        own_rows[a].wait()
        early.append([first_out(a, c)])
    for a in (0, 1):
        rows_over[a].wait_recv()
        early[a].append(first_out(a, 1 - c))
        join(lambda core, a=a: t_in.at[core, a], a, OWN)
        to_across[a, OWN] = message(block(a, OWN), block(a, ACROSS), z_across)
        if a == 1:
            to_right[1, OWN] = [message(block(1, OWN, cols), block(1, LEFT, cols), x_right) for cols in parts]
            to_left[0, OWN] = [message(block(0, OWN, cols), block(0, RIGHT, cols), x_left) for cols in parts]
            to_right[1, OWN][0].start()
            to_left[0, OWN][0].start()
        to_across[a, OWN].start()
        over[a, OWN] = hand_over(a, OWN)
    for copy in weights:
        copy.start()

    def relay_far(a):
        if a == 0:
            relay[a] = message(block(a, LEFT), block(a, FAR), x_right)
        else:
            relay[a] = message(block(a, RIGHT), block(a, FAR), x_left)
        relay[a].start()

    def from_across(a):
        to_across[a, OWN].wait_recv()
        to_right[a, ACROSS] = message(block(a, ACROSS), block(a, ACROSS_LEFT), x_right)
        to_left[a, ACROSS] = message(block(a, ACROSS), block(a, ACROSS_RIGHT), x_left)
        to_right[a, ACROSS].start()
        to_left[a, ACROSS].start()
        over[a, ACROSS] = hand_over(a, ACROSS)

    def from_far(a):
        relay[a].wait_recv()
        to_across[a, FAR] = message(block(a, FAR), block(a, ACROSS_FAR), z_across)
        to_across[a, FAR].start()
        over[a, FAR] = hand_over(a, FAR)

    def arrived(copy, a, slot):
        copy.wait_recv()
        over[a, slot] = hand_over(a, slot)

    def wait_over(a, slots):
        for slot in slots:
            over[a, slot].wait_recv()

    def columns(k):
        return pl.ds(pl.multiple_of((c * 2 + k) % 4 * 1024, 1024), 1024)

    def gate_up(r0, count, slots):
        span = pl.ds(r0, count)
        rows = xc[0, span, columns(0)]
        gf[span, :] = mm(rows, wg[columns(0), :])
        uf[span, :] = mm(rows, wu[columns(0), :])

        def step(k):
            ks = columns(k)
            rows = xc[0, span, ks]
            gf[span, :] += mm(rows, wg[ks, :])
            uf[span, :] += mm(rows, wu[ks, :])

        step(1)
        wait_over(0, slots)
        pl.loop(2, 4)(step)

        @pl.loop(0, count // 16)
        def _(i):
            r = pl.ds(pl.multiple_of(r0 + i * 16, 16), 16)
            gate, up = gf[r, :], uf[r, :]
            s = 1.0 / (1.0 + jnp.exp(-gate))
            swish = gate * s
            hid[r, :] = (swish * up).astype(BF16)
            gf[r, :] = up * s * (1.0 + gate * (1.0 - s))
            uf[r, :] = swish

    def backward(r0, count, slots):
        span = pl.ds(0, count)
        df[span, :] = mm_nt(xc[1, r0:r0 + count, columns(0)], wd[:, columns(0)])

        def step(k):
            ks = columns(k)
            df[span, :] += mm_nt(xc[1, r0:r0 + count, ks], wd[:, ks])

        step(1)
        wait_over(1, slots)
        pl.loop(2, 4)(step)

        @pl.loop(0, count // 16)
        def _(i):
            r = pl.ds(pl.multiple_of(r0 + i * 16, 16), 16)
            dhidden = df[pl.ds(pl.multiple_of(i * 16, 16), 16), :]
            dg[r, :] = (dhidden * gf[r, :]).astype(BF16)
            du[r, :] = (dhidden * uf[r, :]).astype(BF16)

    def mixed_sums():
        @pl.loop(0, 4)
        def _(j):
            cols = pl.ds(pl.multiple_of((1 - c) * HALF + j * PANEL, PANEL), PANEL)
            mb[j] = mm(hid[...], wd[:, cols]).astype(BF16)

        @pl.loop(0, 4)
        def _(j):
            cols = pl.ds(pl.multiple_of(c * HALF + j * PANEL, PANEL), PANEL)
            total = mm(hid[...], wd[:, cols]).astype(BF16)
            am[:, pl.ds(pl.multiple_of(j * PANEL, PANEL), PANEL)] = total

    def transpose(q, src, start, stop):
        for i in range(start, stop):
            lt[q * PANEL:(q + 1) * PANEL, i * 128:(i + 1) * 128] = src[i * 128:(i + 1) * 128, :].T

    def first_in(a, slot):
        for copy in early[a]:
            copy.wait_recv()
        join(lambda core: t_next.at[a, core], a, slot)

    first_in(0, LEFT)
    relay_far(0)
    to_right[1, OWN][1].start()
    first_in(1, RIGHT)
    relay_far(1)
    to_left[0, OWN][1].start()
    over[0, LEFT] = hand_over(0, LEFT)
    over[1, RIGHT] = hand_over(1, RIGHT)
    from_across(0)
    from_across(1)
    weights[0].wait()
    weights[1].wait()
    gate_up(0, FIRST, (OWN, LEFT, ACROSS))
    from_far(0)
    from_far(1)
    for a, slot, halves in ((0, RIGHT, to_left[0, OWN]), (1, LEFT, to_right[1, OWN])):
        halves[0].wait_recv()
        arrived(halves[1], a, slot)
    gate_up(FIRST, MOST - FIRST, (RIGHT, FAR))
    weights[2].wait()
    backward(0, MOST, (OWN, LEFT, ACROSS, RIGHT, FAR))
    for q, src in enumerate((dg, du, hid)):
        transpose(q, src, 0, 3)
    distant = (ACROSS_LEFT, ACROSS_RIGHT, ACROSS_FAR)
    for a in (0, 1):
        arrived(to_left[a, ACROSS], a, ACROSS_RIGHT)
        arrived(to_right[a, ACROSS], a, ACROSS_LEFT)
        arrived(to_across[a, FAR], a, ACROSS_FAR)
        if a == 0:
            gate_up(MOST, ROWS - MOST, distant)
    backward(MOST, ROWS - MOST, distant)
    gather = list(pending)

    def place(z, yr):
        d = ((zl + z) % 2) * 4 + (y + yr) % 4
        return pl.ds(pl.multiple_of(d * PANEL, PANEL), PANEL)

    def grad_term(z, source, rows):
        if source < 0:
            return mm(lt[rows, :], xc[0, :, place(z, 0)])
        cols = pl.ds(pl.multiple_of((zl + z) % 2 * PANEL, PANEL), PANEL)
        return mm(lty[source, rows, :], ry[source, :, cols])

    def quarter(lane, part):
        return pl.ds(lane * PANEL + part * QROWS, QROWS)

    def grad_down(z, yr):
        total = mm(lt[2 * PANEL:, :], xc[1, :, place(z, yr)]).astype(BF16)
        if z:
            pdo[yr] = total
        else:
            wd[:, yr * PANEL:(yr + 1) * PANEL] = total

    class Ring:
        def __init__(self, own, spare, right, left, rows, step):
            self.own, self.spare, self.right, self.left = own, spare, right, left
            self.rows, self.step = rows, step

        def far_lane(self, lane):
            copy = message(self.own(lane, 2), self.spare(0, lane), (self.right, self.left)[lane])
            setattr(self, ("far0", "far1")[lane], copy)
            copy.start()

        def far(self):
            self.far_lane(0)
            self.far_lane(1)

        def near(self):
            own, spare = self.own, self.spare
            self.near1 = message(own(1, 1), spare(1, 1), self.right)
            self.near0 = message(own(0, 3), spare(1, 0), self.left)
            self.near1.start()
            self.near0.start()

        def pass_on(self):
            own, spare = self.own, self.spare
            self.far0.wait_recv()
            add_into(own(0, 1), spare(0, 0), self.rows, self.step)
            self.last0 = message(own(0, 1), spare(2, 0), self.right)
            self.last0.start()
            self.far1.wait_recv()
            add_into(own(1, 3), spare(0, 1), self.rows, self.step)
            self.last1 = message(own(1, 3), spare(2, 1), self.left)
            self.last1.start()

        def finish(self, lane, extra=()):
            (self.near0, self.near1)[lane].wait_recv()
            (self.last0, self.last1)[lane].wait_recv()
            spare = self.spare
            mine = self.own(lane, 0)
            sum_to(mine, (mine, spare(1, lane), spare(2, lane)) + tuple(extra), self.rows, self.step)

    def down_ring(n, own):
        return Ring(own, lambda kind, lane: dring.at[n, kind, lane], y_right, y_left, QROWS // 2, 64)

    def lower(lane):
        return pl.ds(QROWS + lane * (QROWS // 2), QROWS // 2)

    down_a = down_ring(0, lambda lane, yr: wd.at[pl.ds(lane * (QROWS // 2), QROWS // 2), pl.ds(yr * PANEL, PANEL)])
    down_b = [
        down_ring(1, lambda lane, yr: wd.at[lower(lane), pl.ds(yr * PANEL, PANEL)]),
        down_ring(2, lambda lane, yr: pdo.at[yr, lower(lane), :]),
    ]

    slot_of = ((OWN, RIGHT, FAR, LEFT), (ACROSS, ACROSS_RIGHT, ACROSS_FAR, ACROSS_LEFT))

    def token_rows(m, slot, cols):
        rows = pl.ds(slot * BLOCK, BLOCK)
        return am.at[rows, cols] if m == 0 else xc.at[1, rows, cols]

    def token_ring(m, z):
        return Ring(
            lambda lane, xr: token_rows(m, slot_of[z][xr], pl.ds(lane * LANE, LANE)),
            lambda kind, lane: mring.at[m, z, kind, lane],
            x_right, x_left, BLOCK, 16,
        )

    tr = {(m, z): token_ring(m, z) for m in (0, 1) for z in (0, 1)}

    def half(ref, lane):
        return ref.at[pl.ds(lane * PANEL, PANEL), :]

    l_right = [message(half(lt, lane), half(lty.at[2], lane), y_right) for lane in (0, 1)]
    l_left = [message(half(lt, lane), half(lty.at[0], lane), y_left) for lane in (0, 1)]
    transpose(0, dg, 3, 5)
    l_right[0].start()
    transpose(1, du, 3, 5)
    l_left[1].start()
    l_right[1].start()
    l_left[0].start()
    transpose(2, hid, 3, 5)
    down_z = {}
    for yr in (2, 1, 3, 0):
        grad_down(1, yr)
        down_z[yr] = message(pdo.at[yr, pl.ds(0, QROWS), :], dz.at[yr], z_next)
        down_z[yr].start()
    mixed_sums()
    mixed_over = [message(mb.at[j], sm.at[j], sibling) for j in range(4)]
    for copy in mixed_over:
        copy.start()
    for yr in (2, 1, 3, 0):
        grad_down(0, yr)
    for j in range(4):
        mixed_over[j].wait_recv()
        add_into(am.at[:, pl.ds(j * PANEL, PANEL)], sm.at[j], ROWS, 64)
    pl.semaphore_signal(credit, inc=1, device_id=sibling, device_id_type=MESH)
    tr[0, 1].far()
    tr[0, 1].near()
    for copy in gather:
        wait_send(copy)

    def input_grad(base, j):
        w = pl.ds(pl.multiple_of(base * HALF + j * PANEL, PANEL), PANEL)
        return (mm_nt(dg[...], wg[w, :]) + mm_nt(du[...], wu[w, :])).astype(BF16)

    @pl.loop(0, 4)
    def _(j):
        xc[1, :, pl.ds(pl.multiple_of(HALF + j * PANEL, PANEL), PANEL)] = input_grad(1 - c, j)

    pl.semaphore_wait(credit, 1)
    ig_over = [message(xc.at[1, :, pl.ds(HALF + j * PANEL, PANEL)], sm.at[j], sibling) for j in range(4)]
    for copy in ig_over:
        copy.start()
    tr[0, 1].pass_on()

    @pl.loop(0, 4)
    def _(j):
        xc[1, :, pl.ds(pl.multiple_of(j * PANEL, PANEL), PANEL)] = input_grad(c, j)

    token_z = {}

    def send_across(m):
        for lane in (0, 1):
            tr[m, 1].finish(lane)
        token_z[m] = message(token_rows(m, ACROSS, pl.ds(0, HALF)), mz.at[m], z_across)
        token_z[m].start()

    l_far = {}
    for lane, source, device in ((0, 2, y_right), (1, 0, y_left)):
        (l_right, l_left)[lane][lane].wait_recv()
        for part in (0, 1):
            rows = quarter(lane, part)
            l_far[lane, part] = message(lty.at[source, rows, :], lty.at[1, rows, :], device)
            l_far[lane, part].start()
    for j in range(4):
        ig_over[j].wait_recv()
        add_into(xc.at[1, :, pl.ds(j * PANEL, PANEL)], sm.at[j], ROWS, 64)
    tr[1, 1].far()
    tr[1, 1].near()
    down_b[1].far()
    down_b[1].near()
    send_across(0)
    r_over = []
    for source in (0, 2, 1):
        for slot in range(8):
            r_sent[3 - source, slot].wait_recv()
        columns_held = ry.at[source, :, r_half]
        copy = message(columns_held, columns_held, sibling)
        copy.start()
        r_over.append(copy)

    def accumulate(source, rows):
        acc[rows, :] = grad_term(1, source, rows) if source < 0 else acc[rows, :] + grad_term(1, source, rows)

    for lane in (0, 1):
        accumulate(-1, pl.ds(lane * PANEL, PANEL))

    def down_step(yr):
        down_z[yr].wait_recv()
        add_into(wd.at[pl.ds(0, QROWS), pl.ds(yr * PANEL, PANEL)], dz.at[yr], QROWS, 64)

    tr[1, 1].pass_on()
    for m in (0, 1):
        tr[m, 0].far()
        tr[m, 0].near()
    for copy in r_over:
        copy.wait_recv()
    l_left[0].wait_recv()
    l_right[1].wait_recv()
    for source in (0, 2):
        for lane in (0, 1):
            accumulate(source, pl.ds(lane * PANEL, PANEL))
    send_across(1)
    gate_z = {}
    for part in (0, 1):
        for lane in (0, 1):
            rows = quarter(lane, part)
            l_far[lane, part].wait_recv()
            gzs[rows, :] = (acc[rows, :] + grad_term(1, 1, rows)).astype(BF16)
            gate_z[lane, part] = message(gzs.at[rows, :], gz.at[rows, :], z_next)
            gate_z[lane, part].start()
    down_b[1].pass_on()
    for yr in (2, 1, 3, 0):
        down_step(yr)
    for ring in (down_a, down_b[0]):
        ring.far()
        ring.near()
    for m in (0, 1):
        tr[m, 0].pass_on()

    @pl.loop(0, 2)
    def _(lane):
        rows = pl.ds(pl.multiple_of(lane * PANEL, PANEL), PANEL)
        acc[rows, :] = grad_term(0, -1, rows) + grad_term(0, 0, rows) + grad_term(0, 1, rows) + grad_term(0, 2, rows)

    for lane in (0, 1):
        down_b[1].finish(lane)
    down_b_z = message(pdo.at[0, pl.ds(QROWS, QROWS), :], dbz, z_next)
    down_b_z.start()
    down_a.pass_on()
    down_b[0].pass_on()

    outs = []
    for m, out in enumerate((mixed_out, ig_out)):
        for lane in (0, 1):
            tr[m, 0].finish(lane)
        token_z[m].wait_recv()
        rows = token_rows(m, OWN, pl.ds(0, HALF))

        @pl.loop(0, 4)
        def _(j, m=m, rows=rows):
            cols = pl.ds(pl.multiple_of(j * PANEL, PANEL), PANEL)
            total = rows[:, cols].astype(F32) + mz[m, :, cols].astype(F32)
            top, bottom = total[:BLOCK // 2], total[BLOCK // 2:]
            fo[m, 0, :, cols] = jnp.where(c == 0, top, bottom).astype(BF16)
            fo[m, 1, :, cols] = jnp.where(c == 0, bottom, top).astype(BF16)

        keep = pltpu.make_async_copy(fo.at[m, 0], out.at[:, mine], local_sem.at[5 + m])
        give = message(fo.at[m, 1], out.at[:, mine], sibling)
        keep.start()
        give.start()
        outs.append((keep, give))

    grads = []
    for part in (0, 1):
        for lane in (0, 1):
            rows = quarter(lane, part)
            gate_z[lane, part].wait_recv()
            total = (acc[rows, :] + gz[rows, :].astype(F32)).astype(BF16)
            fin[lane, :, part * QROWS:(part + 1) * QROWS] = total.T
    for lane, out in enumerate((gate_out, up_out)):
        copy = pltpu.make_async_copy(fin.at[lane], out, local_sem.at[7 + lane])
        copy.start()
        grads.append(copy)
    for lane in (0, 1):
        down_a.finish(lane)
    down_b_z.wait_recv()
    for lane in (0, 1):
        down_b[0].finish(lane, (dbz.at[pl.ds(lane * (QROWS // 2), QROWS // 2), :],))
    copy = pltpu.make_async_copy(wd.at[:, pl.ds(0, PANEL)], down_out, local_sem.at[9])
    copy.start()
    grads.append(copy)

    for keep, give in outs:
        keep.wait()
        give.wait_recv()
    for copy in grads:
        copy.wait()
    for copy in pending:
        wait_send(copy)


def arrange(*refs):
    sources, results, held, sem = refs[:5], refs[5:10], refs[10:15], refs[15]
    ins = [pltpu.make_async_copy(sources[n], held[n], sem.at[n]) for n in range(5)]
    outs = [pltpu.make_async_copy(held[n], results[n], sem.at[5 + n]) for n in range(5)]
    for copy in ins:
        copy.start()
    for n in range(5):
        ins[n].wait()
        outs[n].start()
    for copy in outs:
        copy.wait()


def on_device(tokens, w_gate, w_up, w_down, cotangent):
    v = lambda *shape: pltpu.VMEM(shape, BF16)
    shapes = [jax.ShapeDtypeStruct((BLOCK // 2, D), BF16)] * 2 + [jax.ShapeDtypeStruct((PANEL, PANEL), BF16)] * 3
    results = pl.pallas_call(
        kernel,
        out_shape=shapes,
        in_specs=[pl.BlockSpec(memory_space=pl.ANY)] * 5,
        out_specs=[pl.BlockSpec(memory_space=pl.ANY)] * 5,
        scratch_shapes=[
            v(D, PANEL), v(D, PANEL), v(PANEL, D),
            v(2, ROWS, D),
            v(ROWS, PANEL), v(ROWS, PANEL), v(ROWS, PANEL),
            v(3 * PANEL, ROWS),
            pltpu.VMEM((ROWS, PANEL), F32), pltpu.VMEM((ROWS, PANEL), F32), pltpu.VMEM((MOST, PANEL), F32),
            v(ROWS, HALF), v(4, ROWS, PANEL), v(4, ROWS, PANEL), v(4, PANEL, PANEL),
            v(2, 2, 3, 2, BLOCK, LANE), v(2, BLOCK, HALF),
            v(3, ROWS, 2 * PANEL), v(3, 2 * PANEL, ROWS),
            pltpu.VMEM((2 * PANEL, PANEL), F32), v(2 * PANEL, PANEL), v(2 * PANEL, PANEL), v(2, PANEL, PANEL),
            v(4, QROWS, PANEL), v(QROWS, PANEL), v(3, 3, 2, QROWS // 2, PANEL),
            v(2, 2, BLOCK // 2, HALF), v(2, 2, BLOCK // 2, HALF), v(2, 2, BLOCK // 2, HALF),
            pltpu.SemaphoreType.DMA((MESSAGES,)),
            pltpu.SemaphoreType.DMA((MESSAGES,)),
            pltpu.SemaphoreType.DMA((10,)),
            pltpu.SemaphoreType.REGULAR,
        ],
        compiler_params=pltpu.CompilerParams(
            collective_id=0, has_side_effects=True, vmem_limit_bytes=63 * 1024 * 1024
        ),
        cost_estimate=pl.CostEstimate(flops=24_200_000_000, bytes_accessed=16_000_000, transcendentals=330_000),
    )(tokens, w_gate, w_up, w_down, cotangent)
    return pl.pallas_call(
        arrange,
        out_shape=shapes,
        in_specs=[pl.BlockSpec(memory_space=pl.ANY)] * 5,
        out_specs=[pl.BlockSpec(memory_space=pl.ANY)] * 5,
        scratch_shapes=[pltpu.VMEM(shape.shape, BF16) for shape in shapes] + [pltpu.SemaphoreType.DMA((10,))],
        compiler_params=pltpu.CompilerParams(vmem_limit_bytes=60 * 1024 * 1024),
    )(*results)


def solution(mesh):
    in_specs = (
        P(("dp", "mp"), None),
        P(None, "mp"),
        P(None, "mp"),
        P("mp", None),
        P(("dp", "mp"), None),
    )
    out_specs = (
        P(("dp", "mp"), None),
        P(("dp", "mp"), None),
        P("dp", "mp"),
        P("dp", "mp"),
        P("mp", "dp"),
    )
    return jax.shard_map(
        on_device, mesh=mesh, in_specs=in_specs, out_specs=out_specs, check_vma=False
    )
```

```python
import jax
import jax.numpy as jnp
from jax import lax
from jax.experimental import pallas as pl
from jax.experimental.pallas import tpu as pltpu
from jax.sharding import PartitionSpec as P

MESH = pl.DeviceIdType.MESH
BF16 = jnp.bfloat16
F32 = jnp.float32
D = 4096
HALF = D // 2
LANE = HALF // 2
PANEL = 512
ROWS = 640
BLOCK = 80
FIRST = 240
MOST = 400
MESSAGES = 160
QROWS = PANEL // 2

OWN, LEFT, ACROSS, RIGHT, FAR, ACROSS_LEFT, ACROSS_RIGHT, ACROSS_FAR = range(8)


def mm(a, b):
    return jnp.dot(a, b, preferred_element_type=F32)


def mm_nt(a, b):
    return lax.dot_general(a, b, (((1,), (1,)), ((), ())), preferred_element_type=F32)


def add_into(dst, src, rows, step):
    @pl.loop(0, rows // step)
    def _(i):
        r = pl.ds(pl.multiple_of(i * step, step), step)
        dst[r, :] = (dst[r, :].astype(F32) + src[r, :].astype(F32)).astype(BF16)


def sum_to(dst, terms, rows, step):
    @pl.loop(0, rows // step)
    def _(i):
        r = pl.ds(pl.multiple_of(i * step, step), step)
        total = terms[0][r, :].astype(F32)
        for term in terms[1:]:
            total += term[r, :].astype(F32)
        dst[r, :] = total.astype(BF16)


def kernel(
    tok_hbm, wg_hbm, wu_hbm, wd_hbm, cot_hbm,
    mixed_out, ig_out, gate_out, up_out, down_out,
    wg, wu, wd, xc, hid, dg, du, lt, gf, uf, df, am, mb, sm, pdo,
    mring, mz, ry, lty, acc, gzs, gz, fin, dz, dbz, dring, t_in, t_next, fo,
    send_sem, recv_sem, local_sem, credit,
):
    dp, mp = lax.axis_index("dp"), lax.axis_index("mp")
    zl, y = dp // 4, dp % 4
    zh, x, c = mp // 8, (mp // 2) % 4, mp % 2
    x_right = (dp, zh * 8 + ((x + 1) % 4) * 2 + c)
    x_left = (dp, zh * 8 + ((x + 3) % 4) * 2 + c)
    z_across = (dp, (1 - zh) * 8 + x * 2 + c)
    sibling = (dp, zh * 8 + x * 2 + (1 - c))
    y_right = (zl * 4 + (y + 1) % 4, mp)
    y_left = (zl * 4 + (y + 3) % 4, mp)
    y_far = (zl * 4 + (y + 2) % 4, mp)
    z_next = ((1 - zl) * 4 + y, mp)
    mine = pl.ds(pl.multiple_of(c * HALF, HALF), HALF)
    other = pl.ds(pl.multiple_of((1 - c) * HALF, HALF), HALF)

    pending = []

    def message(src, dst, device):
        n = len(pending)
        copy = pltpu.make_async_remote_copy(
            src_ref=src, dst_ref=dst, send_sem=send_sem.at[n], recv_sem=recv_sem.at[n],
            device_id=device, device_id_type=MESH,
        )
        pending.append(copy)
        return copy

    sent = set()

    def wait_send(copy):
        if id(copy) not in sent:
            sent.add(id(copy))
            copy.wait_send()

    weights = [
        pltpu.make_async_copy(src, dst, local_sem.at[n])
        for n, (src, dst) in enumerate(((wg_hbm, wg), (wu_hbm, wu), (wd_hbm, wd)))
    ]
    inputs = (tok_hbm, cot_hbm)
    own_rows = [pltpu.make_async_copy(inputs[a].at[:, mine], t_in.at[c, a], local_sem.at[3 + a]) for a in (0, 1)]
    for copy in own_rows:
        copy.start()

    barrier = pltpu.get_barrier_semaphore()
    partners = (x_right, x_left, z_across, sibling, y_right, y_left, y_far, z_next)
    for device in partners:
        pl.semaphore_signal(barrier, inc=1, device_id=device, device_id_type=MESH)
    pl.semaphore_wait(barrier, len(partners))

    rows_over = [message(inputs[a].at[:, other], t_in.at[c, a], sibling) for a in (0, 1)]
    for copy in rows_over:
        copy.start()

    def block(a, slot, cols=mine):
        return xc.at[a, pl.ds(slot * BLOCK, BLOCK), cols]

    r_half = pl.ds(pl.multiple_of(c * PANEL, PANEL), PANEL)
    r_sent = {}

    def send_columns(slot):
        rows = pl.ds(slot * BLOCK, BLOCK)
        for yr, device in ((1, y_right), (3, y_left), (2, y_far)):
            cols = pl.ds(pl.multiple_of(c * HALF + (y + yr) % 4 * PANEL, PANEL), PANEL)
            r_sent[yr, slot] = message(xc.at[0, rows, cols], ry.at[3 - yr, rows, r_half], device)
            r_sent[yr, slot].start()

    def hand_over(a, slot):
        copy = message(block(a, slot), block(a, slot), sibling)
        copy.start()
        if a == 0:
            send_columns(slot)
        return copy

    parts = [pl.ds(pl.multiple_of(c * HALF + i * LANE, LANE), LANE) for i in (0, 1)]
    to_right, to_left, to_across, relay, over = {}, {}, {}, {}, {}

    def first_out(a, core):
        copy = message(t_in.at[core, a], t_next.at[a, core], (x_right, x_left)[a])
        copy.start()
        return copy

    def join(halves, a, slot):
        @pl.loop(0, HALF // PANEL)
        def _(j):
            cols = pl.ds(pl.multiple_of(j * PANEL, PANEL), PANEL)
            both = jnp.concatenate([halves(0)[:, cols].astype(F32), halves(1)[:, cols].astype(F32)], axis=0)
            to = pl.ds(pl.multiple_of(c * HALF + j * PANEL, PANEL), PANEL)
            xc[a, slot * BLOCK:(slot + 1) * BLOCK, to] = both.astype(BF16)

    early = []
    for a in (0, 1):
        own_rows[a].wait()
        early.append([first_out(a, c)])
    for a in (0, 1):
        rows_over[a].wait_recv()
        early[a].append(first_out(a, 1 - c))
        join(lambda core, a=a: t_in.at[core, a], a, OWN)
        to_across[a, OWN] = message(block(a, OWN), block(a, ACROSS), z_across)
        if a == 1:
            to_right[1, OWN] = [message(block(1, OWN, cols), block(1, LEFT, cols), x_right) for cols in parts]
            to_left[0, OWN] = [message(block(0, OWN, cols), block(0, RIGHT, cols), x_left) for cols in parts]
            to_right[1, OWN][0].start()
            to_left[0, OWN][0].start()
        to_across[a, OWN].start()
        over[a, OWN] = hand_over(a, OWN)
    for copy in weights:
        copy.start()

    def relay_far(a):
        if a == 0:
            relay[a] = message(block(a, LEFT), block(a, FAR), x_right)
        else:
            relay[a] = message(block(a, RIGHT), block(a, FAR), x_left)
        relay[a].start()

    def from_across(a):
        to_across[a, OWN].wait_recv()
        to_right[a, ACROSS] = message(block(a, ACROSS), block(a, ACROSS_LEFT), x_right)
        to_left[a, ACROSS] = message(block(a, ACROSS), block(a, ACROSS_RIGHT), x_left)
        to_right[a, ACROSS].start()
        to_left[a, ACROSS].start()
        over[a, ACROSS] = hand_over(a, ACROSS)

    def from_far(a):
        relay[a].wait_recv()
        to_across[a, FAR] = message(block(a, FAR), block(a, ACROSS_FAR), z_across)
        to_across[a, FAR].start()
        over[a, FAR] = hand_over(a, FAR)

    def arrived(copy, a, slot):
        copy.wait_recv()
        over[a, slot] = hand_over(a, slot)

    def wait_over(a, slots):
        for slot in slots:
            over[a, slot].wait_recv()

    def columns(k):
        return pl.ds(pl.multiple_of((c * 2 + k) % 4 * 1024, 1024), 1024)

    def gate_up(r0, count, slots):
        span = pl.ds(r0, count)
        rows = xc[0, span, columns(0)]
        gf[span, :] = mm(rows, wg[columns(0), :])
        uf[span, :] = mm(rows, wu[columns(0), :])

        def step(k):
            ks = columns(k)
            rows = xc[0, span, ks]
            gf[span, :] += mm(rows, wg[ks, :])
            uf[span, :] += mm(rows, wu[ks, :])

        step(1)
        wait_over(0, slots)
        pl.loop(2, 4)(step)

        @pl.loop(0, count // 16)
        def _(i):
            r = pl.ds(pl.multiple_of(r0 + i * 16, 16), 16)
            gate, up = gf[r, :], uf[r, :]
            s = 1.0 / (1.0 + jnp.exp(-gate))
            swish = gate * s
            hid[r, :] = (swish * up).astype(BF16)
            gf[r, :] = up * s * (1.0 + gate * (1.0 - s))
            uf[r, :] = swish

    def backward(r0, count, slots):
        span = pl.ds(0, count)
        df[span, :] = mm_nt(xc[1, r0:r0 + count, columns(0)], wd[:, columns(0)])

        def step(k):
            ks = columns(k)
            df[span, :] += mm_nt(xc[1, r0:r0 + count, ks], wd[:, ks])

        step(1)
        wait_over(1, slots)
        pl.loop(2, 4)(step)

        @pl.loop(0, count // 16)
        def _(i):
            r = pl.ds(pl.multiple_of(r0 + i * 16, 16), 16)
            dhidden = df[pl.ds(pl.multiple_of(i * 16, 16), 16), :]
            dg[r, :] = (dhidden * gf[r, :]).astype(BF16)
            du[r, :] = (dhidden * uf[r, :]).astype(BF16)

    def mixed_sums():
        @pl.loop(0, 4)
        def _(j):
            cols = pl.ds(pl.multiple_of((1 - c) * HALF + j * PANEL, PANEL), PANEL)
            mb[j] = mm(hid[...], wd[:, cols]).astype(BF16)

        @pl.loop(0, 4)
        def _(j):
            cols = pl.ds(pl.multiple_of(c * HALF + j * PANEL, PANEL), PANEL)
            total = mm(hid[...], wd[:, cols]).astype(BF16)
            am[:, pl.ds(pl.multiple_of(j * PANEL, PANEL), PANEL)] = total

    def transpose(q, src, start, stop):
        for i in range(start, stop):
            lt[q * PANEL:(q + 1) * PANEL, i * 128:(i + 1) * 128] = src[i * 128:(i + 1) * 128, :].T

    def first_in(a, slot):
        for copy in early[a]:
            copy.wait_recv()
        join(lambda core: t_next.at[a, core], a, slot)

    first_in(0, LEFT)
    relay_far(0)
    to_right[1, OWN][1].start()
    first_in(1, RIGHT)
    relay_far(1)
    to_left[0, OWN][1].start()
    over[0, LEFT] = hand_over(0, LEFT)
    over[1, RIGHT] = hand_over(1, RIGHT)
    from_across(0)
    from_across(1)
    weights[0].wait()
    weights[1].wait()
    gate_up(0, FIRST, (OWN, LEFT, ACROSS))
    from_far(0)
    from_far(1)
    for a, slot, halves in ((0, RIGHT, to_left[0, OWN]), (1, LEFT, to_right[1, OWN])):
        halves[0].wait_recv()
        arrived(halves[1], a, slot)
    gate_up(FIRST, MOST - FIRST, (RIGHT, FAR))
    weights[2].wait()

    def arrived_across(a):
        arrived(to_across[a, FAR], a, ACROSS_FAR)
        arrived(to_left[a, ACROSS], a, ACROSS_RIGHT)
        arrived(to_right[a, ACROSS], a, ACROSS_LEFT)

    distant = (ACROSS_LEFT, ACROSS_RIGHT, ACROSS_FAR)
    arrived_across(0)
    backward(0, MOST, (OWN, LEFT, ACROSS, RIGHT, FAR))
    gate_up(MOST, ROWS - MOST, distant)
    arrived_across(1)
    for q, src in enumerate((dg, du, hid)):
        transpose(q, src, 0, 3)
    backward(MOST, ROWS - MOST, distant)
    gather = list(pending)

    def place(z, yr):
        d = ((zl + z) % 2) * 4 + (y + yr) % 4
        return pl.ds(pl.multiple_of(d * PANEL, PANEL), PANEL)

    def grad_term(z, source, rows):
        if source < 0:
            return mm(lt[rows, :], xc[0, :, place(z, 0)])
        cols = pl.ds(pl.multiple_of((zl + z) % 2 * PANEL, PANEL), PANEL)
        return mm(lty[source, rows, :], ry[source, :, cols])

    def quarter(lane, part):
        return pl.ds(lane * PANEL + part * QROWS, QROWS)

    def grad_down(z, yr):
        total = mm(lt[2 * PANEL:, :], xc[1, :, place(z, yr)]).astype(BF16)
        if z:
            pdo[yr] = total
        else:
            wd[:, yr * PANEL:(yr + 1) * PANEL] = total

    class Ring:
        def __init__(self, own, spare, right, left, rows, step):
            self.own, self.spare, self.right, self.left = own, spare, right, left
            self.rows, self.step = rows, step

        def far_lane(self, lane):
            copy = message(self.own(lane, 2), self.spare(0, lane), (self.right, self.left)[lane])
            setattr(self, ("far0", "far1")[lane], copy)
            copy.start()

        def far(self):
            self.far_lane(0)
            self.far_lane(1)

        def near(self):
            own, spare = self.own, self.spare
            self.near1 = message(own(1, 1), spare(1, 1), self.right)
            self.near0 = message(own(0, 3), spare(1, 0), self.left)
            self.near1.start()
            self.near0.start()

        def pass_on(self):
            own, spare = self.own, self.spare
            self.far0.wait_recv()
            add_into(own(0, 1), spare(0, 0), self.rows, self.step)
            self.last0 = message(own(0, 1), spare(2, 0), self.right)
            self.last0.start()
            self.far1.wait_recv()
            add_into(own(1, 3), spare(0, 1), self.rows, self.step)
            self.last1 = message(own(1, 3), spare(2, 1), self.left)
            self.last1.start()

        def finish(self, lane, extra=()):
            (self.near0, self.near1)[lane].wait_recv()
            (self.last0, self.last1)[lane].wait_recv()
            spare = self.spare
            mine = self.own(lane, 0)
            sum_to(mine, (mine, spare(1, lane), spare(2, lane)) + tuple(extra), self.rows, self.step)

    def down_ring(n, own):
        return Ring(own, lambda kind, lane: dring.at[n, kind, lane], y_right, y_left, QROWS // 2, 64)

    def lower(lane):
        return pl.ds(QROWS + lane * (QROWS // 2), QROWS // 2)

    down_a = down_ring(0, lambda lane, yr: wd.at[pl.ds(lane * (QROWS // 2), QROWS // 2), pl.ds(yr * PANEL, PANEL)])
    down_b = [
        down_ring(1, lambda lane, yr: wd.at[lower(lane), pl.ds(yr * PANEL, PANEL)]),
        down_ring(2, lambda lane, yr: pdo.at[yr, lower(lane), :]),
    ]

    slot_of = ((OWN, RIGHT, FAR, LEFT), (ACROSS, ACROSS_RIGHT, ACROSS_FAR, ACROSS_LEFT))

    def token_rows(m, slot, cols):
        rows = pl.ds(slot * BLOCK, BLOCK)
        return am.at[rows, cols] if m == 0 else xc.at[1, rows, cols]

    def token_ring(m, z):
        return Ring(
            lambda lane, xr: token_rows(m, slot_of[z][xr], pl.ds(lane * LANE, LANE)),
            lambda kind, lane: mring.at[m, z, kind, lane],
            x_right, x_left, BLOCK, 16,
        )

    tr = {(m, z): token_ring(m, z) for m in (0, 1) for z in (0, 1)}

    def half(ref, lane):
        return ref.at[pl.ds(lane * PANEL, PANEL), :]

    l_right = [message(half(lt, lane), half(lty.at[2], lane), y_right) for lane in (0, 1)]
    l_left = [message(half(lt, lane), half(lty.at[0], lane), y_left) for lane in (0, 1)]
    transpose(0, dg, 3, 5)
    l_right[0].start()
    transpose(1, du, 3, 5)
    l_left[1].start()
    l_right[1].start()
    l_left[0].start()
    transpose(2, hid, 3, 5)
    down_z = {}
    for yr in (2, 1, 3, 0):
        grad_down(1, yr)
        down_z[yr] = message(pdo.at[yr, pl.ds(0, QROWS), :], dz.at[yr], z_next)
        down_z[yr].start()
    mixed_sums()
    mixed_over = [message(mb.at[j], sm.at[j], sibling) for j in range(4)]
    for copy in mixed_over:
        copy.start()
    for yr in (2, 1, 3, 0):
        grad_down(0, yr)
    for j in range(4):
        mixed_over[j].wait_recv()
        add_into(am.at[:, pl.ds(j * PANEL, PANEL)], sm.at[j], ROWS, 64)
    pl.semaphore_signal(credit, inc=1, device_id=sibling, device_id_type=MESH)
    tr[0, 1].far()
    tr[0, 1].near()
    for copy in gather:
        wait_send(copy)

    def input_grad(base, j):
        w = pl.ds(pl.multiple_of(base * HALF + j * PANEL, PANEL), PANEL)
        return (mm_nt(dg[...], wg[w, :]) + mm_nt(du[...], wu[w, :])).astype(BF16)

    @pl.loop(0, 4)
    def _(j):
        xc[1, :, pl.ds(pl.multiple_of(HALF + j * PANEL, PANEL), PANEL)] = input_grad(1 - c, j)

    pl.semaphore_wait(credit, 1)
    ig_over = [message(xc.at[1, :, pl.ds(HALF + j * PANEL, PANEL)], sm.at[j], sibling) for j in range(4)]
    for copy in ig_over:
        copy.start()
    tr[0, 1].pass_on()

    @pl.loop(0, 4)
    def _(j):
        xc[1, :, pl.ds(pl.multiple_of(j * PANEL, PANEL), PANEL)] = input_grad(c, j)

    token_z = {}

    def send_across(m):
        for lane in (0, 1):
            tr[m, 1].finish(lane)
        token_z[m] = message(token_rows(m, ACROSS, pl.ds(0, HALF)), mz.at[m], z_across)
        token_z[m].start()

    l_far = {}
    for lane, source, device in ((0, 2, y_right), (1, 0, y_left)):
        (l_right, l_left)[lane][lane].wait_recv()
        for part in (0, 1):
            rows = quarter(lane, part)
            l_far[lane, part] = message(lty.at[source, rows, :], lty.at[1, rows, :], device)
            l_far[lane, part].start()
    for j in range(4):
        ig_over[j].wait_recv()
        add_into(xc.at[1, :, pl.ds(j * PANEL, PANEL)], sm.at[j], ROWS, 64)
    tr[1, 1].far()
    tr[1, 1].near()
    down_b[1].far()
    down_b[1].near()
    send_across(0)
    r_over = []
    for source in (0, 2, 1):
        for slot in range(8):
            r_sent[3 - source, slot].wait_recv()
        columns_held = ry.at[source, :, r_half]
        copy = message(columns_held, columns_held, sibling)
        copy.start()
        r_over.append(copy)

    def accumulate(source, rows):
        acc[rows, :] = grad_term(1, source, rows) if source < 0 else acc[rows, :] + grad_term(1, source, rows)

    for lane in (0, 1):
        accumulate(-1, pl.ds(lane * PANEL, PANEL))

    def down_step(yr):
        down_z[yr].wait_recv()
        add_into(wd.at[pl.ds(0, QROWS), pl.ds(yr * PANEL, PANEL)], dz.at[yr], QROWS, 64)

    tr[1, 1].pass_on()
    for m in (0, 1):
        tr[m, 0].far()
        tr[m, 0].near()
    for copy in r_over:
        copy.wait_recv()
    l_left[0].wait_recv()
    l_right[1].wait_recv()
    for source in (0, 2):
        for lane in (0, 1):
            accumulate(source, pl.ds(lane * PANEL, PANEL))
    send_across(1)
    gate_z = {}
    for part in (0, 1):
        for lane in (0, 1):
            rows = quarter(lane, part)
            l_far[lane, part].wait_recv()
            gzs[rows, :] = (acc[rows, :] + grad_term(1, 1, rows)).astype(BF16)
            gate_z[lane, part] = message(gzs.at[rows, :], gz.at[rows, :], z_next)
            gate_z[lane, part].start()
    down_b[1].pass_on()
    for yr in (2, 1, 3, 0):
        down_step(yr)
    for ring in (down_a, down_b[0]):
        ring.far()
        ring.near()
    for m in (0, 1):
        tr[m, 0].pass_on()

    @pl.loop(0, 2)
    def _(lane):
        rows = pl.ds(pl.multiple_of(lane * PANEL, PANEL), PANEL)
        acc[rows, :] = grad_term(0, -1, rows) + grad_term(0, 0, rows) + grad_term(0, 1, rows) + grad_term(0, 2, rows)

    for lane in (0, 1):
        down_b[1].finish(lane)
    down_b_z = message(pdo.at[0, pl.ds(QROWS, QROWS), :], dbz, z_next)
    down_b_z.start()
    down_a.pass_on()
    down_b[0].pass_on()

    outs = []
    for m, out in enumerate((mixed_out, ig_out)):
        for lane in (0, 1):
            tr[m, 0].finish(lane)
        token_z[m].wait_recv()
        rows = token_rows(m, OWN, pl.ds(0, HALF))

        @pl.loop(0, 4)
        def _(j, m=m, rows=rows):
            cols = pl.ds(pl.multiple_of(j * PANEL, PANEL), PANEL)
            total = rows[:, cols].astype(F32) + mz[m, :, cols].astype(F32)
            top, bottom = total[:BLOCK // 2], total[BLOCK // 2:]
            fo[m, 0, :, cols] = jnp.where(c == 0, top, bottom).astype(BF16)
            fo[m, 1, :, cols] = jnp.where(c == 0, bottom, top).astype(BF16)

        keep = pltpu.make_async_copy(fo.at[m, 0], out.at[:, mine], local_sem.at[5 + m])
        give = message(fo.at[m, 1], out.at[:, mine], sibling)
        keep.start()
        give.start()
        outs.append((keep, give))

    grads = []
    for part in (0, 1):
        for lane in (0, 1):
            rows = quarter(lane, part)
            gate_z[lane, part].wait_recv()
            total = (acc[rows, :] + gz[rows, :].astype(F32)).astype(BF16)
            fin[lane, :, part * QROWS:(part + 1) * QROWS] = total.T
    for lane, out in enumerate((gate_out, up_out)):
        copy = pltpu.make_async_copy(fin.at[lane], out, local_sem.at[7 + lane])
        copy.start()
        grads.append(copy)
    for lane in (0, 1):
        down_a.finish(lane)
    down_b_z.wait_recv()
    for lane in (0, 1):
        down_b[0].finish(lane, (dbz.at[pl.ds(lane * (QROWS // 2), QROWS // 2), :],))
    copy = pltpu.make_async_copy(wd.at[:, pl.ds(0, PANEL)], down_out, local_sem.at[9])
    copy.start()
    grads.append(copy)

    for keep, give in outs:
        keep.wait()
        give.wait_recv()
    for copy in grads:
        copy.wait()
    for copy in pending:
        wait_send(copy)


def arrange(*refs):
    sources, results, held, sem = refs[:5], refs[5:10], refs[10:15], refs[15]
    ins = [pltpu.make_async_copy(sources[n], held[n], sem.at[n]) for n in range(5)]
    outs = [pltpu.make_async_copy(held[n], results[n], sem.at[5 + n]) for n in range(5)]
    for copy in ins:
        copy.start()
    for n in range(5):
        ins[n].wait()
        outs[n].start()
    for copy in outs:
        copy.wait()


def on_device(tokens, w_gate, w_up, w_down, cotangent):
    v = lambda *shape: pltpu.VMEM(shape, BF16)
    shapes = [jax.ShapeDtypeStruct((BLOCK // 2, D), BF16)] * 2 + [jax.ShapeDtypeStruct((PANEL, PANEL), BF16)] * 3
    results = pl.pallas_call(
        kernel,
        out_shape=shapes,
        in_specs=[pl.BlockSpec(memory_space=pl.ANY)] * 5,
        out_specs=[pl.BlockSpec(memory_space=pl.ANY)] * 5,
        scratch_shapes=[
            v(D, PANEL), v(D, PANEL), v(PANEL, D),
            v(2, ROWS, D),
            v(ROWS, PANEL), v(ROWS, PANEL), v(ROWS, PANEL),
            v(3 * PANEL, ROWS),
            pltpu.VMEM((ROWS, PANEL), F32), pltpu.VMEM((ROWS, PANEL), F32), pltpu.VMEM((MOST, PANEL), F32),
            v(ROWS, HALF), v(4, ROWS, PANEL), v(4, ROWS, PANEL), v(4, PANEL, PANEL),
            v(2, 2, 3, 2, BLOCK, LANE), v(2, BLOCK, HALF),
            v(3, ROWS, 2 * PANEL), v(3, 2 * PANEL, ROWS),
            pltpu.VMEM((2 * PANEL, PANEL), F32), v(2 * PANEL, PANEL), v(2 * PANEL, PANEL), v(2, PANEL, PANEL),
            v(4, QROWS, PANEL), v(QROWS, PANEL), v(3, 3, 2, QROWS // 2, PANEL),
            v(2, 2, BLOCK // 2, HALF), v(2, 2, BLOCK // 2, HALF), v(2, 2, BLOCK // 2, HALF),
            pltpu.SemaphoreType.DMA((MESSAGES,)),
            pltpu.SemaphoreType.DMA((MESSAGES,)),
            pltpu.SemaphoreType.DMA((10,)),
            pltpu.SemaphoreType.REGULAR,
        ],
        compiler_params=pltpu.CompilerParams(
            collective_id=0, has_side_effects=True, vmem_limit_bytes=63 * 1024 * 1024
        ),
        cost_estimate=pl.CostEstimate(flops=24_200_000_000, bytes_accessed=16_000_000, transcendentals=330_000),
    )(tokens, w_gate, w_up, w_down, cotangent)
    return pl.pallas_call(
        arrange,
        out_shape=shapes,
        in_specs=[pl.BlockSpec(memory_space=pl.ANY)] * 5,
        out_specs=[pl.BlockSpec(memory_space=pl.ANY)] * 5,
        scratch_shapes=[pltpu.VMEM(shape.shape, BF16) for shape in shapes] + [pltpu.SemaphoreType.DMA((10,))],
        compiler_params=pltpu.CompilerParams(vmem_limit_bytes=60 * 1024 * 1024),
    )(*results)


def solution(mesh):
    in_specs = (
        P(("dp", "mp"), None),
        P(None, "mp"),
        P(None, "mp"),
        P("mp", None),
        P(("dp", "mp"), None),
    )
    out_specs = (
        P(("dp", "mp"), None),
        P(("dp", "mp"), None),
        P("dp", "mp"),
        P("dp", "mp"),
        P("mp", "dp"),
    )
    return jax.shard_map(
        on_device, mesh=mesh, in_specs=in_specs, out_specs=out_specs, check_vma=False
    )
```
